256 devices in a mesh: dp: 16 (over z_lo, y, core), tensor: 16 (over x, z_hi).
Axes of the slice: x: 4, y: 4, z: 8 (z_hi: 4, z_lo: 2; z = z_hi * 2 + z_lo), core: 2. Of those that a mesh axis runs over, the one named last changes fastest.
Arguments:
- saved_codes: bfloat16 [3072, 4096], P(('dp', 'tensor')), may hold values from -24 to 24
- saved_scales: bfloat16 [3072, 32], P(('dp', 'tensor')), may hold values from 0.25 to 4
- gate_weight: bfloat16 [4096, 14336], P('dp', 'tensor'), may hold values from -0.09375 to 0.09375
- up_weight: bfloat16 [4096, 14336], P('dp', 'tensor'), may hold values from -0.09375 to 0.09375
- hidden_grad: bfloat16 [3072, 14336], P('dp', 'tensor'), may hold values from -6 to 6
Outputs:
- input_grad: bfloat16 [3072, 4096], P(('dp', 'tensor'))
- gate_grad: float32 [4096, 14336], P('dp', 'tensor')
- up_grad: float32 [4096, 14336], P('dp', 'tensor')
The draws below stay inside these ranges and needn't reach their ends.
All inputs are finite; a program needn't handle non-finite values.
Results may differ from the reference program's by a relative error of at most 0.02.
Values may be sent and summed in bfloat16 or wider, within the bound.
No kernel may reach another device: no remote copies, remote signals or barrier semaphores. Data moves between devices by JAX's collectives and lax.ppermute only.
A program may use at most 128 MiB of HBM per device.

```python
import math
import jax
import jax.numpy as jnp
from jax import lax

D = 4096
FF = 14336
QBLOCK = 128
TOK_GRP = 192
TOKENS = 3072
N_DP = 16
N_TENSOR = 16


def strengthened(entries, rng, source, target, shards_of, factor):
    def block_of(axis_at):
        return (jnp.arange(entries.shape[axis_at]) // (entries.shape[axis_at] // shards_of)).reshape((-1,) + (1,) * (entries.ndim - 1 - axis_at))

    near = jax.random.permutation(rng, shards_of)[block_of(target)]
    second = (block_of(target) + shards_of // 2) % shards_of
    return jnp.where((block_of(source) == near) | (block_of(source) == second), factor * entries, entries)


def steps_of(stream_key, shape, cuts, smallest, top_value):
    def one(position, shards_of):
        steps = jax.random.uniform(jax.random.fold_in(jax.random.fold_in(stream_key, 6), position), (shards_of,), jnp.float32, smallest / len(cuts), top_value / len(cuts))
        return jnp.repeat(jnp.exp(steps), shape[position] // shards_of).reshape((-1,) + (1,) * (len(shape) - position - 1))

    loudness = one(*cuts[0])
    for cut in cuts[1:]:
        loudness = loudness * one(*cut)
    return loudness


def gaussian(own_key, shape, width, bound, cuts=(), dtype=jnp.bfloat16):
    drawn = width * jax.random.normal(own_key, shape, jnp.float32)
    if cuts:
        drawn = drawn * steps_of(own_key, shape, cuts, -0.22, 0.18)
    return jnp.clip(drawn, -bound, bound).astype(dtype)


def heavy_noise(rng, shape, scale, bound, split, heavy, held_as=jnp.bfloat16):
    values = scale * jax.random.normal(rng, shape, jnp.float32)
    if split:
        values = values * steps_of(rng, shape, split, -0.22, 0.18)
    return jnp.clip(strengthened(values, jax.random.fold_in(rng, 3), *heavy), -bound, bound).astype(held_as)


def setup_inputs(seed: int = 0) -> dict:
    splits = jax.random.split(jax.random.key(seed), 6)
    saved_codes = heavy_noise(splits[0], (TOKENS, D), 1.0, 24.0, ((0, 256),), (0, 1, 256, 6.0))
    saved_scales = jnp.clip(jnp.exp(math.log(4.0) - 2.7725887 * jax.random.uniform(splits[1], (TOKENS, D // QBLOCK), jnp.float32) ** steps_of(splits[1], (TOKENS, D // QBLOCK), ((0, 256),), -0.2, 0.2)), 0.25, 4.0).astype(jnp.bfloat16)
    gate_weight = gaussian(splits[2], (D, FF), D ** -0.5, 0.09375, ((0, 16), (1, 16)))
    up_weight = gaussian(splits[3], (D, FF), D ** -0.5, 0.09375, ((0, 16), (1, 16)))
    hidden_grad = heavy_noise(splits[4], (TOKENS, FF), 1.0, 6.0, ((0, 16), (1, 16)), (1, 0, 16, 2.0))
    return {"saved_codes": saved_codes, "saved_scales": saved_scales, "gate_weight": gate_weight, "up_weight": up_weight, "hidden_grad": hidden_grad}


def dequantize(code_rows, scale_rows):
    row_count, features = code_rows.shape
    blocks = scale_rows.shape[1]
    values = code_rows.astype(jnp.float32).reshape(row_count, blocks, features // blocks) * scale_rows.astype(jnp.float32)[:, :, None]
    return values.reshape(row_count, features).astype(jnp.bfloat16)


def reference(saved_codes, saved_scales, gate_weight, up_weight, hidden_grad):
    inputs = dequantize(saved_codes, saved_scales)
    hidden_share = FF // N_TENSOR
    gate_blocks = gate_weight.astype(jnp.float32).reshape(D, N_TENSOR, hidden_share)
    up_blocks = up_weight.astype(jnp.float32).reshape(D, N_TENSOR, hidden_share)

    def one_group(running, slabs):
        group_inputs, group_grad = slabs
        gate_sum = jnp.dot(group_inputs, gate_weight, preferred_element_type=jnp.float32)
        up_sum = jnp.dot(group_inputs, up_weight, preferred_element_type=jnp.float32)
        gate_sigmoid = jax.nn.sigmoid(gate_sum)
        upstream = group_grad.astype(jnp.float32)
        grad_gate = (upstream * up_sum * gate_sigmoid * (1.0 + gate_sum * (1.0 - gate_sigmoid))).astype(jnp.bfloat16)
        grad_up = (upstream * gate_sum * gate_sigmoid).astype(jnp.bfloat16)
        gate_parts = grad_gate.astype(jnp.float32).reshape(TOK_GRP, N_TENSOR, hidden_share)
        up_parts = grad_up.astype(jnp.float32).reshape(TOK_GRP, N_TENSOR, hidden_share)
        block_terms = jnp.einsum("tkf,dkf->ktd", gate_parts, gate_blocks) + jnp.einsum("tkf,dkf->ktd", up_parts, up_blocks)
        block_terms = lax.optimization_barrier(block_terms.astype(jnp.bfloat16)).astype(jnp.float32)
        input_part = jnp.sum(block_terms, axis=0).astype(jnp.bfloat16)
        gate_term = jnp.dot(group_inputs.T, grad_gate, preferred_element_type=jnp.float32) / TOK_GRP
        up_term = jnp.dot(group_inputs.T, grad_up, preferred_element_type=jnp.float32) / TOK_GRP
        gate_term = lax.optimization_barrier(gate_term.astype(jnp.bfloat16)).astype(jnp.float32)
        up_term = lax.optimization_barrier(up_term.astype(jnp.bfloat16)).astype(jnp.float32)
        return (running[0] + gate_term, running[1] + up_term), input_part

    zeros = jnp.zeros((D, FF), jnp.float32)
    slabs = (inputs.reshape(N_DP, TOK_GRP, D), hidden_grad.reshape(N_DP, TOK_GRP, FF))
    (gate_grad, up_grad), input_parts = lax.scan(one_group, (zeros, zeros), slabs)
    return input_parts.reshape(TOKENS, D), gate_grad, up_grad
```

```python
import itertools

import jax
import jax.numpy as jnp
from jax import lax
from jax.experimental import pallas as pl
from jax.experimental.pallas import tpu as pltpu
from jax.sharding import PartitionSpec as P

BOTH = ("dp", "tensor")
F32 = jnp.float32
BF16 = jnp.bfloat16
CHUNKS = (512, 384)


def perm(target):
    def index(zl, y, c, x, zh):
        return (((zl % 2) * 4 + y % 4) * 2 + c % 2) * 16 + (x % 4) * 4 + zh % 4

    return [
        (index(*at), index(*target(*at, 1 - 2 * at[2])))
        for at in itertools.product(range(2), range(4), range(2), range(4), range(4))
    ]


TO_CORE = perm(lambda zl, y, c, x, zh, s: (zl, y, c + 1, x, zh))
TO_ZL = perm(lambda zl, y, c, x, zh, s: (zl + 1, y, c, x, zh))
Y_UP = perm(lambda zl, y, c, x, zh, s: (zl, y + s, c, x, zh))
Y_DOWN = perm(lambda zl, y, c, x, zh, s: (zl, y - s, c, x, zh))
X_UP = perm(lambda zl, y, c, x, zh, s: (zl, y, c, x + s, zh))
X_DOWN = perm(lambda zl, y, c, x, zh, s: (zl, y, c, x - s, zh))
ZH_UP = perm(lambda zl, y, c, x, zh, s: (zl, y, c, x, zh + s))
ZH_DOWN = perm(lambda zl, y, c, x, zh, s: (zl, y, c, x, zh - s))


def send(value, pairs):
    return lax.ppermute(value, BOTH, pairs)


def ring_gather(value, up, down):
    below = send(value, up)
    above = send(value, down)
    far = send(below, up)
    return [value, below, above, far]


def ring_sum(pieces, up, down):
    own, below, above, far = pieces
    passed = send(far(None).astype(BF16), down)
    direct = send(above(None).astype(BF16), up)
    merged = send(below(passed).astype(BF16), down)
    return own(direct) + merged.astype(F32)


def plus(value, arrived):
    return value if arrived is None else value + arrived.astype(F32)


def offsets(s):
    return (0, -s, s, 2)


def dequantize_kernel(order, codes, scales, own, other, values):
    blocks = scales.shape[1]
    width = codes.shape[1] // blocks
    for b in range(blocks):
        at = slice(b * width, (b + 1) * width)
        values[:, at] = (codes[:, at].astype(F32) * scales[:, b : b + 1].astype(F32)).astype(BF16)
    for k in range(8):
        at = slice(k * 256, (k + 1) * 256)
        own[:, at] = values[:, pl.ds(pl.multiple_of(order[k] * 256, 256), 256)]
        other[:, at] = values[:, pl.ds(pl.multiple_of(order[8 + k] * 256, 256), 256)]


def dequantize(codes, scales, order):
    rows, features = codes.shape
    half = jax.ShapeDtypeStruct((rows, features // 2), BF16)
    vmem = pl.BlockSpec(memory_space=pltpu.VMEM)
    return pl.pallas_call(
        dequantize_kernel,
        out_shape=(half, half),
        in_specs=[pl.BlockSpec(memory_space=pltpu.SMEM), vmem, vmem],
        out_specs=(vmem, vmem),
        scratch_shapes=[pltpu.VMEM((rows, features), BF16)],
    )(order, codes, scales)


def restore_kernel(order, own, other, out):
    for k in range(8):
        at = slice(k * 256, (k + 1) * 256)
        out[:, pl.ds(pl.multiple_of(order[k] * 256, 256), 256)] = own[:, at]
        out[:, pl.ds(pl.multiple_of(order[8 + k] * 256, 256), 256)] = other[:, at]


def restore(own, other, order):
    rows, half = own.shape
    vmem = pl.BlockSpec(memory_space=pltpu.VMEM)
    return pl.pallas_call(
        restore_kernel,
        out_shape=jax.ShapeDtypeStruct((rows, 2 * half), BF16),
        in_specs=[pl.BlockSpec(memory_space=pltpu.SMEM), vmem, vmem],
        out_specs=vmem,
    )(order, own, other)


def local(saved_codes, saved_scales, gate_weight, up_weight, hidden_grad):
    dp, tensor = lax.axis_index("dp"), lax.axis_index("tensor")
    zl, y, c = dp // 8, (dp // 2) % 4, dp % 2
    x, zh = tensor // 4, tensor % 4
    s = 1 - 2 * c
    rows = saved_codes.shape[0]
    group = hidden_grad.shape[0]

    cuts = list(itertools.accumulate((0,) + CHUNKS))
    spans = [slice(2 * a, 2 * b) for a, b in itertools.pairwise(cuts)]
    shard = jnp.concatenate(
        [w[:, a:b] for a, b in itertools.pairwise(cuts) for w in (gate_weight, up_weight)], axis=1
    )
    mine = ring_gather(shard, Y_UP, Y_DOWN)
    pieces = mine + [send(piece, TO_CORE) for piece in mine]

    blocks = [((y + d) % 4) * 2 + c for d in offsets(s)] + [((y + d) % 4) * 2 + 1 - c for d in offsets(-s)]
    order = jnp.stack([zl * 8 + b for b in blocks] + [(1 - zl) * 8 + b for b in blocks]).astype(jnp.int32)
    kept, given = dequantize(saved_codes, saved_scales, order)
    pair = jnp.concatenate([kept, send(given, TO_ZL)], axis=0)
    column = ring_gather(pair, ZH_UP, ZH_DOWN)
    slab = jnp.concatenate([p[:rows] for p in column] + [p[rows:] for p in column], axis=0)
    plane = ring_gather(slab, X_UP, X_DOWN)
    quarter = 4 * rows
    inputs = jnp.concatenate([p[:quarter] for p in plane] + [p[quarter:] for p in plane], axis=0)
    features = [inputs[:, 256 * k : 256 * (k + 1)] for k in range(8)]

    places = jnp.stack([((x + a) % 4) * 4 + (zh + b) % 4 for a in offsets(s) for b in offsets(s)])
    source = (places[:, None] * rows + jnp.arange(rows)[None, :]).reshape(group, 1)
    pick = (source == jnp.arange(group)[None, :]).astype(BF16)
    upstream = jnp.dot(pick, hidden_grad, preferred_element_type=F32)

    grads = []
    for size, span, start in zip(CHUNKS, spans, cuts):
        partial = sum(
            jnp.dot(f, p[:, span], preferred_element_type=F32) for f, p in zip(features, pieces)
        )
        arrived = send(partial[group:].astype(BF16), TO_ZL)
        total = partial[:group] + arrived.astype(F32)
        gate, up = total[:, :size], total[:, size:]
        sigmoid = jax.nn.sigmoid(gate)
        up_stream = upstream[:, start : start + size]
        grad_gate = (up_stream * up * sigmoid * (1.0 + gate * (1.0 - sigmoid))).astype(BF16)
        grad_up = (up_stream * gate * sigmoid).astype(BF16)
        own = jnp.concatenate([grad_gate, grad_up], axis=1)
        grads.append(jnp.concatenate([own, send(own, TO_ZL)], axis=0))

    by_features = (((1,), (1,)), ((), ()))
    back = jnp.concatenate(
        [
            sum(
                lax.dot_general(g, p[:, span], by_features, preferred_element_type=F32)
                for g, span in zip(grads, spans)
            ).astype(BF16)
            for p in pieces
        ],
        axis=1,
    )
    planes = [
        jnp.concatenate([back[quarter * k : quarter * (k + 1)], back[group + quarter * k : group + quarter * (k + 1)]])
        for k in range(4)
    ]
    slab = ring_sum([lambda a, p=p: plus(p.astype(F32), a) for p in planes], X_UP, X_DOWN)
    columns = [
        jnp.concatenate([slab[rows * k : rows * (k + 1)], slab[quarter + rows * k : quarter + rows * (k + 1)]])
        for k in range(4)
    ]
    pair = ring_sum([lambda a, p=p: plus(p, a) for p in columns], ZH_UP, ZH_DOWN).astype(BF16)
    input_grad = restore(pair[:rows], send(pair[rows:], TO_ZL), order)

    by_tokens = (((0,), (0,)), ((), ()))
    summed = []
    for grad in grads:

        def product(k, grad=grad):
            return lax.dot_general(features[k], grad, by_tokens, preferred_element_type=F32)

        def piece(k):
            shown = send(product(4 + k).astype(BF16), TO_CORE)
            return lambda arrived: plus(plus(product(k), shown), arrived)

        far, above, below, own = (piece(k) for k in (3, 2, 1, 0))
        summed.append(ring_sum([own, below, above, far], Y_UP, Y_DOWN) / group)
    gate_grad = jnp.concatenate([g[:, :size] for g, size in zip(summed, CHUNKS)], axis=1)
    up_grad = jnp.concatenate([g[:, size:] for g, size in zip(summed, CHUNKS)], axis=1)
    return input_grad, gate_grad, up_grad


def solution(mesh):
    placed = (P(BOTH, None), P(BOTH, None), P("dp", "tensor"), P("dp", "tensor"), P("dp", "tensor"))
    return jax.shard_map(
        local,
        mesh=mesh,
        in_specs=placed,
        out_specs=(P(BOTH, None), P("dp", "tensor"), P("dp", "tensor")),
        check_vma=False,
    )
```

```python
import functools
import itertools

import jax
import jax.numpy as jnp
from jax import lax
from jax.experimental import pallas as pl
from jax.experimental.pallas import tpu as pltpu
from jax.sharding import PartitionSpec as P

BOTH = ("dp", "tensor")
F32 = jnp.float32
BF16 = jnp.bfloat16
CHUNKS = (512, 384)
TILE = 256
VMEM_LIMIT = 32 * 1024 * 1024
VMEM = pl.BlockSpec(memory_space=pltpu.VMEM)
ANY = pl.BlockSpec(memory_space=pl.ANY)


def perm(target):
    def index(zl, y, c, x, zh):
        return ((zl * 4 + y) * 2 + c) * 16 + x * 4 + zh

    return [
        (index(*at), index(*target(*at, 3 if at[2] else 1, 1 if at[2] else 3)))
        for at in itertools.product(range(2), range(4), range(2), range(4), range(4))
    ]


TO_CORE = perm(lambda zl, y, c, x, zh, a, b: (zl, y, 1 - c, x, zh))
TO_ZL = perm(lambda zl, y, c, x, zh, a, b: (1 - zl, y, c, x, zh))
Y_A = perm(lambda zl, y, c, x, zh, a, b: (zl, y ^ a, c, x, zh))
Y_B = perm(lambda zl, y, c, x, zh, a, b: (zl, y ^ b, c, x, zh))
X_A = perm(lambda zl, y, c, x, zh, a, b: (zl, y, c, x ^ a, zh))
X_B = perm(lambda zl, y, c, x, zh, a, b: (zl, y, c, x ^ b, zh))
ZH_A = perm(lambda zl, y, c, x, zh, a, b: (zl, y, c, x, zh ^ a))
ZH_B = perm(lambda zl, y, c, x, zh, a, b: (zl, y, c, x, zh ^ b))


def send(value, pairs):
    return lax.ppermute(value, BOTH, pairs)


def fence(*values):
    return lax.optimization_barrier(values)


def call(kernel, out_shape, in_specs, out_specs, scratch=(), cost=None):
    return pl.pallas_call(
        kernel,
        out_shape=out_shape,
        in_specs=in_specs,
        out_specs=out_specs,
        scratch_shapes=list(scratch),
        cost_estimate=cost,
        compiler_params=pltpu.CompilerParams(vmem_limit_bytes=VMEM_LIMIT),
    )


def array(shape, dtype):
    return jax.ShapeDtypeStruct(shape, dtype)


def join_kernel(gate, up, out, sems):
    width = gate.shape[1]
    copies = [
        pltpu.make_async_copy(gate, out.at[:, :width], sems.at[0]),
        pltpu.make_async_copy(up, out.at[:, width:], sems.at[1]),
    ]
    for copy in copies:
        copy.start()
    for copy in copies:
        copy.wait()


def join(gate, up):
    rows, width = gate.shape
    return call(
        join_kernel, array((rows, 2 * width), BF16), [ANY, ANY], ANY, [pltpu.SemaphoreType.DMA((2,))]
    )(gate, up)


def dequantize_kernel(order, codes, scales, own, other, values):
    blocks = scales.shape[1]
    width = codes.shape[1] // blocks
    for b in range(blocks):
        at = slice(b * width, (b + 1) * width)
        values[:, at] = (codes[:, at].astype(F32) * scales[:, b : b + 1].astype(F32)).astype(BF16)
    for k in range(8):
        at = slice(k * 256, (k + 1) * 256)
        own[:, at] = values[:, pl.ds(pl.multiple_of(order[k] * 256, 256), 256)]
        other[:, at] = values[:, pl.ds(pl.multiple_of(order[8 + k] * 256, 256), 256)]


def dequantize(codes, scales, order):
    rows, features = codes.shape
    half = array((rows, features // 2), BF16)
    smem = pl.BlockSpec(memory_space=pltpu.SMEM)
    return call(
        dequantize_kernel, (half, half), [smem, VMEM, VMEM], (VMEM, VMEM), [pltpu.VMEM((rows, features), BF16)]
    )(order, codes, scales)


def restore_kernel(order, own, other, out):
    for k in range(8):
        at = slice(k * 256, (k + 1) * 256)
        out[:, pl.ds(pl.multiple_of(order[k] * 256, 256), 256)] = own[:, at]
        out[:, pl.ds(pl.multiple_of(order[8 + k] * 256, 256), 256)] = other[:, at]


def restore(own, other, order):
    rows, half = own.shape
    smem = pl.BlockSpec(memory_space=pltpu.SMEM)
    return call(restore_kernel, array((rows, 2 * half), BF16), [smem, VMEM, VMEM], VMEM)(order, own, other)


def tiles_of(start, size, hidden):
    tiles = []
    for base in (start, hidden + start):
        for at in range(base, base + size, TILE):
            tiles.append((at, min(TILE, base + size - at)))
    return tiles


def forward_kernel(tiles, split, *refs):
    if split:
        near, away, *refs = refs
    else:
        rows, *refs = refs
    weights, refs = refs[:8], refs[8:]
    if split:
        rows, own, par, held, sems = refs
    else:
        own, par, held, sems = refs
    copies = []
    at = 0
    for t, (start, size) in enumerate(tiles):
        for k in range(8):
            copy = pltpu.make_async_copy(
                weights[k].at[:, start : start + size],
                held.at[256 * k : 256 * (k + 1), at : at + size],
                sems.at[t, k],
            )
            copy.start()
            copies.append(copy)
        at += size
    group = own.shape[0]
    if split:
        part = group // 4
        for n, ref in enumerate((near, away)):
            for q in range(2):
                rows[(2 * n + q) * part : (2 * n + q + 1) * part, :] = ref[2 * q * part : (2 * q + 1) * part, :]
                rows[group + (2 * n + q) * part : group + (2 * n + q + 1) * part, :] = ref[
                    (2 * q + 1) * part : (2 * q + 2) * part, :
                ]
    at = 0
    for t, (start, size) in enumerate(tiles):
        for k in range(8):
            copies[8 * t + k].wait()
        result = jnp.dot(rows[...], held[:, at : at + size], preferred_element_type=F32)
        own[:, at : at + size] = result[:group]
        par[:, at : at + size] = result[group:].astype(BF16)
        at += size


def forward(inputs, weights, start, size, group):
    split = len(inputs) == 2
    hidden = weights[0].shape[1] // 2
    tiles = tiles_of(start, size, hidden)
    width = inputs[0].shape[1]
    outs = (array((group, 2 * size), F32), array((group, 2 * size), BF16))
    if split:
        outs = (array((2 * group, width), BF16),) + outs
    return call(
        functools.partial(forward_kernel, tiles, split),
        outs,
        [VMEM] * len(inputs) + [ANY] * 8,
        (VMEM,) * len(outs),
        [pltpu.VMEM((width, 2 * size), BF16), pltpu.SemaphoreType.DMA((len(tiles), 8))],
        pl.CostEstimate(
            flops=8 * group * width * size, bytes_accessed=4 * width * size + 4 * group * width, transcendentals=0
        ),
    )(*inputs, *weights)


def backward_kernel(chunks, *refs):
    parts, refs = refs[: 2 * len(chunks)], refs[2 * len(chunks) :]
    weights, (out, grads, held, sems) = refs[:8], refs[8:]
    copies = [pltpu.make_async_copy(weights[k], held.at[k], sems.at[k]) for k in range(8)]
    for copy in copies:
        copy.start()
    group = parts[0].shape[0]
    part = group // 4
    hidden = held.shape[2] // 2
    start = 0
    for n, size in enumerate(chunks):
        for z in range(2):
            for q in range(4):
                rows = slice((2 * q + z) * part, (2 * q + z + 1) * part)
                for m in range(2):
                    grads[rows, m * hidden + start : m * hidden + start + size] = parts[2 * n + z][
                        q * part : (q + 1) * part, m * size : (m + 1) * size
                    ]
        start += size
    for k in range(8):
        copies[k].wait()
        out[:, 256 * k : 256 * (k + 1)] = lax.dot_general(
            grads[...], held[k], (((1,), (1,)), ((), ())), preferred_element_type=F32
        ).astype(BF16)


def backward(parts, weights, chunks):
    group = parts[0].shape[0]
    width = weights[0].shape[1]
    return call(
        functools.partial(backward_kernel, chunks),
        array((2 * group, 2048), BF16),
        [VMEM] * len(parts) + [ANY] * 8,
        VMEM,
        [
            pltpu.VMEM((2 * group, width), BF16),
            pltpu.VMEM((8, 256, width), BF16),
            pltpu.SemaphoreType.DMA((8,)),
        ],
        pl.CostEstimate(flops=8 * group * 1024 * width, bytes_accessed=4096 * width, transcendentals=0),
    )(*parts, *weights)


def add(*values):
    total = values[0].astype(F32)
    for value in values[1:]:
        total = total + value.astype(F32)
    return total


def local(saved_codes, saved_scales, gate_weight, up_weight, hidden_grad):
    dp, tensor = lax.axis_index("dp"), lax.axis_index("tensor")
    zl, y, c = dp // 8, (dp // 2) % 4, dp % 2
    x, zh = tensor // 4, tensor % 4
    a, b = 1 + 2 * c, 3 - 2 * c
    rows = saved_codes.shape[0]
    group = hidden_grad.shape[0]

    def places(p, first, second):
        return (p, p ^ first, p ^ second, p ^ 2)

    shard = join(gate_weight, up_weight)
    from_a = send(shard, Y_A)
    from_b = send(shard, Y_B)
    from_ab = send(from_a, Y_B)
    mine = [shard, from_a, from_b, from_ab]
    weights = mine + [send(piece, TO_CORE) for piece in mine]

    blocks = [p * 2 + c for p in places(y, a, b)] + [p * 2 + 1 - c for p in places(y, b, a)]
    order = jnp.stack([zl * 8 + k for k in blocks] + [(1 - zl) * 8 + k for k in blocks]).astype(jnp.int32)
    kept, given = dequantize(saved_codes, saved_scales, order)
    pair = jnp.concatenate([kept, send(given, TO_ZL)], axis=0)
    (pair,) = fence(pair)
    two = jnp.concatenate([pair, send(pair, ZH_A)], axis=0)
    (two,) = fence(two)
    four = jnp.concatenate([two, send(two, ZH_B)], axis=0)
    slab = four.reshape(4, 2, rows, -1).swapaxes(0, 1).reshape(8 * rows, -1)
    (slab,) = fence(slab)
    near = jnp.concatenate([slab, send(slab, X_A)], axis=0)
    (near,) = fence(near)
    away = send(near, X_B)

    at = jnp.stack([p * 4 + q for p in places(x, a, b) for q in places(zh, a, b)])
    source = (at[:, None] * rows + jnp.arange(rows)[None, :]).reshape(group, 1)
    pick = (source == jnp.arange(group)[None, :]).astype(BF16)
    upstream = jnp.dot(pick, hidden_grad, preferred_element_type=F32)

    parts = []
    start = 0
    inputs = None
    for size in CHUNKS:
        if inputs is None:
            inputs, own, par = forward((near, away), weights, start, size, group)
        else:
            own, par = forward((inputs,), weights, start, size, group)
        total = add(own, send(par, TO_ZL))
        gate, up = total[:, :size], total[:, size:]
        sigmoid = jax.nn.sigmoid(gate)
        stream = upstream[:, start : start + size]
        grad_gate = (stream * up * sigmoid * (1.0 + gate * (1.0 - sigmoid))).astype(BF16)
        grad_up = (stream * gate * sigmoid).astype(BF16)
        grad = jnp.concatenate([grad_gate, grad_up], axis=1)
        (grad,) = fence(grad)
        parts += [grad, send(grad, TO_ZL)]
        start += size

    back = backward(parts, weights, CHUNKS)
    half = 2 * group // 2
    back = add(back[:half], send(back[half:], X_B))
    half = half // 2
    slab = add(back[:half], send(back[half:].astype(BF16), X_A))
    four = slab.reshape(2, 4, rows, -1).swapaxes(0, 1).reshape(8 * rows, -1)
    half = half // 2
    four = add(four[:half], send(four[half:].astype(BF16), ZH_B))
    half = half // 2
    pair = add(four[:half], send(four[half:].astype(BF16), ZH_A)).astype(BF16)
    input_grad = restore(pair[:rows], send(pair[rows:], TO_ZL), order)

    summed = []
    for n in range(len(CHUNKS)):
        grad = jnp.concatenate(parts[2 * n : 2 * n + 2], axis=0)

        def product(first, last, grad=grad):
            return lax.dot_general(
                inputs[:, first:last], grad, (((0,), (0,)), ((), ())), preferred_element_type=F32
            )

        shown = [
            send(product(1024 + first, 1024 + last).astype(BF16), TO_CORE)
            for first, last in ((512, 1024), (256, 512), (0, 256))
        ]
        from_b = send(add(product(512, 1024), shown[0]).astype(BF16), Y_B)
        from_a = send(add(product(256, 512), shown[1], from_b[256:]).astype(BF16), Y_A)
        summed.append(add(product(0, 256), shown[2], from_b[:256], from_a) / group)
    gate_grad = jnp.concatenate([g[:, :size] for g, size in zip(summed, CHUNKS)], axis=1)
    up_grad = jnp.concatenate([g[:, size:] for g, size in zip(summed, CHUNKS)], axis=1)
    return input_grad, gate_grad, up_grad


def solution(mesh):
    placed = (P(BOTH, None), P(BOTH, None), P("dp", "tensor"), P("dp", "tensor"), P("dp", "tensor"))
    return jax.shard_map(
        local,
        mesh=mesh,
        in_specs=placed,
        out_specs=(P(BOTH, None), P("dp", "tensor"), P("dp", "tensor")),
        check_vma=False,
    )
```

```python
import functools
import itertools

import jax
import jax.numpy as jnp
import numpy as np
from jax import lax
from jax.experimental import pallas as pl
from jax.experimental.pallas import tpu as pltpu
from jax.sharding import PartitionSpec as P

BOTH = ("dp", "tensor")
F32 = jnp.float32
BF16 = jnp.bfloat16
CHUNKS = (512, 384)
TILE = 256
VMEM_LIMIT = 16 * 1024 * 1024
VMEM = pl.BlockSpec(memory_space=pltpu.VMEM)
ANY = pl.BlockSpec(memory_space=pl.ANY)


def perm(target):
    def index(zl, y, c, x, zh):
        return ((zl * 4 + y) * 2 + c) * 16 + x * 4 + zh

    return [
        (index(*at), index(*target(*at, 3 if at[2] else 1, 1 if at[2] else 3)))
        for at in itertools.product(range(2), range(4), range(2), range(4), range(4))
    ]


TO_CORE = perm(lambda zl, y, c, x, zh, a, b: (zl, y, 1 - c, x, zh))
TO_ZL = perm(lambda zl, y, c, x, zh, a, b: (1 - zl, y, c, x, zh))
Y_A = perm(lambda zl, y, c, x, zh, a, b: (zl, y ^ a, c, x, zh))
Y_B = perm(lambda zl, y, c, x, zh, a, b: (zl, y ^ b, c, x, zh))
X_A = perm(lambda zl, y, c, x, zh, a, b: (zl, y, c, x ^ a, zh))
X_B = perm(lambda zl, y, c, x, zh, a, b: (zl, y, c, x ^ b, zh))
ZH_A = perm(lambda zl, y, c, x, zh, a, b: (zl, y, c, x, zh ^ a))
ZH_B = perm(lambda zl, y, c, x, zh, a, b: (zl, y, c, x, zh ^ b))


def send(value, pairs):
    return lax.ppermute(value, BOTH, pairs)


def fence(*values):
    return lax.optimization_barrier(values)


def call(kernel, out_shape, in_specs, out_specs, scratch=(), cost=None):
    return pl.pallas_call(
        kernel,
        out_shape=out_shape,
        in_specs=in_specs,
        out_specs=out_specs,
        scratch_shapes=list(scratch),
        cost_estimate=cost,
        compiler_params=pltpu.CompilerParams(vmem_limit_bytes=VMEM_LIMIT),
    )


def in_vmem(value):
    return pltpu.with_memory_space_constraint(value, pltpu.VMEM)


def in_hbm(value):
    return pltpu.with_memory_space_constraint(value, pltpu.HBM)


def array(shape, dtype):
    return jax.ShapeDtypeStruct(shape, dtype)


def join_kernel(gate, up, out, sems):
    width = gate.shape[1]
    copies = [
        pltpu.make_async_copy(gate, out.at[:, :width], sems.at[0]),
        pltpu.make_async_copy(up, out.at[:, width:], sems.at[1]),
    ]
    for copy in copies:
        copy.start()
    for copy in copies:
        copy.wait()


def join(gate, up):
    rows, width = gate.shape
    return call(
        join_kernel, pltpu.VMEM((rows, 2 * width), BF16), [ANY, ANY], VMEM, [pltpu.SemaphoreType.DMA((2,))]
    )(in_hbm(gate), in_hbm(up))


def places(p, first, second):
    return (p, p ^ first, p ^ second, p ^ 2)


def feature_blocks():
    dp = lax.axis_index("dp")
    zl, y, c = dp // 8, (dp // 2) % 4, dp % 2
    a, b = 1 + 2 * c, 3 - 2 * c
    blocks = [p * 2 + c for p in places(y, a, b)] + [p * 2 + 1 - c for p in places(y, b, a)]
    starts = [(zl * 8 + k) * 256 for k in blocks] + [((1 - zl) * 8 + k) * 256 for k in blocks]
    return [pl.ds(pl.multiple_of(start, 256), 256) for start in starts]


def dequantize_kernel(codes, scales, own, other, values):
    blocks = scales.shape[1]
    width = codes.shape[1] // blocks
    for b in range(blocks):
        at = slice(b * width, (b + 1) * width)
        values[:, at] = (codes[:, at].astype(F32) * scales[:, b : b + 1].astype(F32)).astype(BF16)
    spans = feature_blocks()
    for k in range(8):
        at = slice(k * 256, (k + 1) * 256)
        own[:, at] = values[:, spans[k]]
        other[:, at] = values[:, spans[8 + k]]


def dequantize(codes, scales):
    rows, features = codes.shape
    half = array((rows, features // 2), BF16)
    return call(
        dequantize_kernel, (half, half), [VMEM, VMEM], (VMEM, VMEM), [pltpu.VMEM((rows, features), BF16)]
    )(codes, scales)


def restore_kernel(own, other, out):
    spans = feature_blocks()
    for k in range(8):
        at = slice(k * 256, (k + 1) * 256)
        out[:, spans[k]] = own[:, at]
        out[:, spans[8 + k]] = other[:, at]


def restore(own, other):
    rows, half = own.shape
    return call(restore_kernel, array((rows, 2 * half), BF16), [VMEM, VMEM], VMEM)(own, other)


def token_table(rows):
    table = np.zeros((2, 4, 4, 1, 16 * rows), np.int32)
    for c, x, zh in itertools.product(range(2), range(4), range(4)):
        a, b = 1 + 2 * c, 3 - 2 * c
        at = [p * 4 + q for p in places(x, a, b) for q in places(zh, a, b)]
        table[c, x, zh, 0] = (np.array(at)[:, None] * rows + np.arange(rows)).reshape(-1)
    return table.reshape(32, 1, 16 * rows)


def arrange_kernel(table, values, out):
    source = table[lax.axis_index("dp") % 2 * 16 + lax.axis_index("tensor")]
    group = values.shape[0]
    pick = (lax.broadcasted_iota(jnp.int32, (group, group), 0) == source).astype(F32).astype(BF16)
    out[...] = lax.dot_general(
        pick, values[...], (((0,), (0,)), ((), ())), preferred_element_type=F32
    ).astype(BF16)


def arrange(values, rows):
    return call(arrange_kernel, array(values.shape, BF16), [VMEM, VMEM], VMEM)(token_table(rows), values)


def near_kernel(values, *refs):
    weights, (held, own, par, rows, sems) = refs[:8], refs[8:]
    copies = [
        pltpu.make_async_copy(weights[k], held.at[256 * k : 256 * (k + 1)], sems.at[k]) for k in range(8)
    ]
    for copy in copies:
        copy.start()
    split_rows(values, rows)
    for copy in copies:
        copy.wait()
    half = own.shape[0]
    for at in range(0, held.shape[1], TILE):
        span = slice(at, at + TILE)
        result = jnp.dot(rows[...], held[:, span], preferred_element_type=F32)
        own[:, span] = result[:half]
        par[:, span] = result[half:].astype(BF16)


def split_rows(values, rows):
    part = values.shape[0] // 4
    for q in range(2):
        for z in range(2):
            rows[(2 * z + q) * part : (2 * z + q + 1) * part, :] = values[
                (2 * q + z) * part : (2 * q + z + 1) * part, :
            ]


def near_products(values, weights):
    tokens, features = values.shape
    width = weights[0].shape[1]
    outs = (
        pltpu.VMEM((features, width), BF16),
        pltpu.VMEM((tokens // 2, width), F32),
        pltpu.VMEM((tokens // 2, width), BF16),
    )
    scratch = [pltpu.VMEM((tokens, features), BF16), pltpu.SemaphoreType.DMA((8,))]
    return call(near_kernel, outs, [VMEM] + [ANY] * 8, (VMEM,) * 3, scratch)(values, *weights)


def away_kernel(values, held, own, par, rows):
    split_rows(values, rows)
    half = own.shape[0]
    for at in range(0, held.shape[1], TILE):
        span = slice(at, at + TILE)
        result = jnp.dot(rows[...], held[:, span], preferred_element_type=F32)
        own[:, span] = result[:half]
        par[:, span] = result[half:].astype(BF16)


def away_products(values, held):
    tokens, features = values.shape
    width = held.shape[1]
    outs = (array((tokens // 2, width), F32), array((tokens // 2, width), BF16))
    return call(away_kernel, outs, [VMEM, VMEM], (VMEM,) * 2, [pltpu.VMEM((tokens, features), BF16)])(values, held)


def sort_kernel(near, away, out):
    part = near.shape[0] // 4
    for n, values in enumerate((near, away)):
        for q in range(2):
            for z in range(2):
                to = (4 * z + 2 * n + q) * part
                out[to : to + part, :] = values[(2 * q + z) * part : (2 * q + z + 1) * part, :]


def sort_rows(near, away):
    tokens, features = near.shape
    return call(sort_kernel, array((2 * tokens, features), BF16), [VMEM, VMEM], VMEM)(near, away)


def gradient_kernel(start, size, near, near_sent, away, away_sent, upstream, out):
    half = near.shape[0]
    hidden = near.shape[1] // 2
    spans = slice(start, start + size), slice(hidden + start, hidden + start + size)
    for n, (kept, sent) in enumerate(((near, near_sent), (away, away_sent))):
        rows = slice(n * half, (n + 1) * half)
        stream = upstream[rows, spans[0]].astype(F32)
        gate, up = (kept[:, at] + sent[:, at].astype(F32) for at in spans)
        sigmoid = jax.nn.sigmoid(gate)
        out[rows, :size] = (stream * up * sigmoid * (1.0 + gate * (1.0 - sigmoid))).astype(BF16)
        out[rows, size:] = (stream * gate * sigmoid).astype(BF16)


def gradient(start, size, near, near_sent, away, away_sent, upstream):
    return call(
        functools.partial(gradient_kernel, start, size),
        array((upstream.shape[0], 2 * size), BF16),
        [VMEM] * 5,
        VMEM,
    )(near, near_sent, away, away_sent, upstream)


def backward_kernel(chunks, *refs):
    parts, (held, out, grads) = refs[: len(chunks)], refs[len(chunks) :]
    hidden = held.shape[1] // 2
    start = 0
    for part, size in zip(parts, chunks):
        grads[:, start : start + size] = part[:, :size]
        grads[:, hidden + start : hidden + start + size] = part[:, size:]
        start += size
    for k in range(8):
        span = slice(256 * k, 256 * (k + 1))
        out[:, span] = lax.dot_general(
            grads[...], held[span], (((1,), (1,)), ((), ())), preferred_element_type=F32
        ).astype(BF16)


def backward(parts, held, chunks):
    group = parts[0].shape[0]
    features, width = held.shape
    return call(
        functools.partial(backward_kernel, chunks),
        array((group, features), BF16),
        [VMEM] * (len(parts) + 1),
        VMEM,
        [pltpu.VMEM((group, width), BF16)],
    )(*parts, held)


def finish_kernel(chunks, scale, *refs):
    sums, lasts, (gate, up) = refs[: len(chunks)], refs[len(chunks) : 2 * len(chunks)], refs[2 * len(chunks) :]
    start = 0
    for size, total, last in zip(chunks, sums, lasts):
        gate[:, start : start + size] = (total[:, :size] + last[:, :size].astype(F32)) * scale
        up[:, start : start + size] = (total[:, size:] + last[:, size:].astype(F32)) * scale
        start += size


def finish(sums, lasts, chunks, scale):
    out = array((sums[0].shape[0], sum(chunks)), F32)
    return call(
        functools.partial(finish_kernel, chunks, scale), (out, out), [VMEM] * (2 * len(chunks)), (VMEM, VMEM)
    )(*sums, *lasts)


def add(*values):
    total = values[0].astype(F32)
    for value in values[1:]:
        total = total + value.astype(F32)
    return total


def local(saved_codes, saved_scales, gate_weight, up_weight, hidden_grad):
    rows = saved_codes.shape[0]
    group = hidden_grad.shape[0]

    row = np.arange(8 * rows)
    taken = (row // rows % 4 * 2 + row // (4 * rows)) * rows + row % rows
    by_group = np.equal(taken[:, None], row[None, :])

    shard = join(gate_weight, up_weight)
    from_a = send(shard, Y_A)
    from_b = send(shard, Y_B)

    saved_codes, saved_scales, _ = fence(saved_codes, saved_scales, shard)
    kept, given = dequantize(saved_codes, saved_scales)
    pair = jnp.concatenate([kept, send(given, TO_ZL)], axis=0)
    (pair,) = fence(pair)
    two = jnp.concatenate([pair, send(pair, ZH_A)], axis=0)
    (two,) = fence(two)
    four = jnp.concatenate([two, send(two, ZH_B)], axis=0)
    slab = jnp.dot(by_group.astype(BF16), four, preferred_element_type=F32).astype(BF16)
    slab, from_a, from_b = fence(slab, from_a, from_b)
    from_ab = send(from_a, Y_B)
    half = 4 * rows
    first = send(slab[:half], X_A)
    second = send(slab[half:], X_A)
    *mine, _ = fence(shard, from_a, from_b, first)
    theirs = [send(piece, TO_CORE) for piece in mine]
    near = jnp.concatenate([slab, first, second], axis=0)
    (near,) = fence(near)
    half = 8 * rows
    first = send(near[:half], X_B)
    second, *theirs = fence(near[half:], *theirs)
    second = send(second, X_B)
    from_ab, _ = fence(from_ab, first)
    weights = mine + [from_ab] + theirs + [send(from_ab, TO_CORE)]
    upstream = arrange(hidden_grad, rows)

    held, near_own, near_par = near_products(near, weights)
    near_sent = send(near_par, TO_ZL)
    second, _ = fence(second, near_own)
    away = jnp.concatenate([first, second], axis=0)
    (away,) = fence(away)
    away_own, away_par = away_products(away, held)
    away_sent = send(away_par, TO_ZL)
    inputs = sort_rows(near, away)
    near_sent, inputs, away_own = fence(near_sent, inputs, away_own)

    starts = list(itertools.accumulate((0,) + CHUNKS))
    grads = [
        gradient(start, size, near_own, near_sent, away_own, away_sent, upstream)
        for start, size in zip(starts, CHUNKS)
    ]
    others = [send(grads[0], TO_ZL)]
    own_back = backward(grads, held, CHUNKS)
    grads[1], own_back = fence(grads[1], own_back)
    others.append(send(grads[1], TO_ZL))
    half = group // 2
    own_sent = send(own_back[half:], X_B)
    others[0], own_sent = fence(others[0], own_sent)

    stages = []
    for n in range(len(CHUNKS)):
        grad = jnp.concatenate([grads[n], others[n]], axis=0)
        if n == 1:
            back = backward(others, held, CHUNKS)
            back, grad = fence(back, grad)
            back_sent = send(back[half:], X_B)

        def product(first, last, grad=grad):
            return lax.dot_general(
                inputs[:, first:last], grad, (((0,), (0,)), ((), ())), preferred_element_type=F32
            )

        shown = send(product(1024, 2048).astype(BF16), TO_CORE)
        passed = add(product(512, 1024), shown[512:]).astype(BF16)
        if n == 0:
            passed, *others = fence(passed, *others)
        else:
            back_sent, passed = fence(back_sent, passed)
        stages.append((product, shown, send(passed, Y_B)))

    def second_stage(n):
        product, shown, from_b = stages[n]
        return add(product(256, 512), shown[256:512], from_b[256:]).astype(BF16)

    own_back = add(own_back[:half], own_sent)
    back = add(back[:half], back_sent)
    half = half // 2
    given = jnp.concatenate([own_back[half:], back[half:]], axis=0).astype(BF16)
    kept = jnp.concatenate([own_back[:half], back[:half]], axis=0)
    arrived = send(given, X_A)
    passed = [second_stage(0)]
    arrived, passed[0] = fence(arrived, passed[0])
    four = jnp.dot(
        by_group.T.astype(np.float32),
        add(kept, arrived),
        preferred_element_type=F32,
        precision=lax.Precision.HIGHEST,
    )
    half = 4 * rows
    arrived = send(four[half:].astype(BF16), ZH_B)
    passed.append(second_stage(1))
    arrived, passed[1] = fence(arrived, passed[1])
    four = add(four[:half], arrived)
    half = half // 2
    pair = add(four[:half], send(four[half:].astype(BF16), ZH_A)).astype(BF16)
    input_grad = restore(pair[:rows], send(pair[rows:], TO_ZL))

    lasts = [send(value, Y_A) for value in passed]
    sums = [add(product(0, 256), shown[:256], from_b[:256]) for product, shown, from_b in stages]
    gate_grad, up_grad = finish(sums, lasts, CHUNKS, 1.0 / group)
    return input_grad, gate_grad, up_grad


def solution(mesh):
    placed = (P(BOTH, None), P(BOTH, None), P("dp", "tensor"), P("dp", "tensor"), P("dp", "tensor"))
    return jax.shard_map(
        local,
        mesh=mesh,
        in_specs=placed,
        out_specs=(P(BOTH, None), P("dp", "tensor"), P("dp", "tensor")),
        check_vma=False,
    )
```

```python
import functools
import itertools

import jax
import jax.numpy as jnp
import numpy as np
from jax import lax
from jax.experimental import pallas as pl
from jax.experimental.pallas import tpu as pltpu
from jax.sharding import PartitionSpec as P

BOTH = ("dp", "tensor")
F32 = jnp.float32
BF16 = jnp.bfloat16
TILE = 256
VMEM_LIMIT = 16 * 1024 * 1024
VMEM = pl.BlockSpec(memory_space=pltpu.VMEM)
ANY = pl.BlockSpec(memory_space=pl.ANY)


def perm(target):
    def index(zl, y, c, x, zh):
        return ((zl * 4 + y) * 2 + c) * 16 + x * 4 + zh

    return [
        (index(*at), index(*target(*at, 3 if at[2] else 1, 1 if at[2] else 3)))
        for at in itertools.product(range(2), range(4), range(2), range(4), range(4))
    ]


TO_CORE = perm(lambda zl, y, c, x, zh, a, b: (zl, y, 1 - c, x, zh))
TO_ZL = perm(lambda zl, y, c, x, zh, a, b: (1 - zl, y, c, x, zh))
TO_ZL_ZH_A = perm(lambda zl, y, c, x, zh, a, b: (1 - zl, y, c, x, zh ^ a))
Y_A = perm(lambda zl, y, c, x, zh, a, b: (zl, y ^ a, c, x, zh))
Y_B = perm(lambda zl, y, c, x, zh, a, b: (zl, y ^ b, c, x, zh))
X_A = perm(lambda zl, y, c, x, zh, a, b: (zl, y, c, x ^ a, zh))
X_B = perm(lambda zl, y, c, x, zh, a, b: (zl, y, c, x ^ b, zh))
ZH_A = perm(lambda zl, y, c, x, zh, a, b: (zl, y, c, x, zh ^ a))
ZH_B = perm(lambda zl, y, c, x, zh, a, b: (zl, y, c, x, zh ^ b))


def send(value, pairs):
    return lax.ppermute(value, BOTH, pairs)


def fence(*values):
    return lax.optimization_barrier(values)


def call(kernel, out_shape, in_specs, out_specs, scratch=(), cost=None):
    return pl.pallas_call(
        kernel,
        out_shape=out_shape,
        in_specs=in_specs,
        out_specs=out_specs,
        scratch_shapes=list(scratch),
        cost_estimate=cost,
        compiler_params=pltpu.CompilerParams(vmem_limit_bytes=VMEM_LIMIT),
    )


def in_vmem(value):
    return pltpu.with_memory_space_constraint(value, pltpu.VMEM)


def in_hbm(value):
    return pltpu.with_memory_space_constraint(value, pltpu.HBM)


def array(shape, dtype):
    return jax.ShapeDtypeStruct(shape, dtype)


def join_kernel(gate, up, out, sems):
    width = gate.shape[1]
    copies = [
        pltpu.make_async_copy(gate, out.at[:, :width], sems.at[0]),
        pltpu.make_async_copy(up, out.at[:, width:], sems.at[1]),
    ]
    for copy in copies:
        copy.start()
    for copy in copies:
        copy.wait()


def join(gate, up):
    rows, width = gate.shape
    return call(
        join_kernel, pltpu.VMEM((rows, 2 * width), BF16), [ANY, ANY], VMEM, [pltpu.SemaphoreType.DMA((2,))]
    )(in_hbm(gate), in_hbm(up))


def places(p, first, second):
    return (p, p ^ first, p ^ second, p ^ 2)


def feature_blocks():
    dp = lax.axis_index("dp")
    zl, y, c = dp // 8, (dp // 2) % 4, dp % 2
    a, b = 1 + 2 * c, 3 - 2 * c
    blocks = [p * 2 + c for p in places(y, a, b)] + [p * 2 + 1 - c for p in places(y, b, a)]
    starts = [(zl * 8 + k) * 256 for k in blocks] + [((1 - zl) * 8 + k) * 256 for k in blocks]
    return [pl.ds(pl.multiple_of(start, 256), 256) for start in starts]


def dequantize_kernel(codes, scales, own, other, values):
    blocks = scales.shape[1]
    width = codes.shape[1] // blocks
    for b in range(blocks):
        at = slice(b * width, (b + 1) * width)
        values[:, at] = (codes[:, at].astype(F32) * scales[:, b : b + 1].astype(F32)).astype(BF16)
    spans = feature_blocks()
    for k in range(8):
        at = slice(k * 256, (k + 1) * 256)
        own[:, at] = values[:, spans[k]]
        other[:, at] = values[:, spans[8 + k]]


def dequantize(codes, scales):
    rows, features = codes.shape
    half = array((rows, features // 2), BF16)
    return call(
        dequantize_kernel, (half, half), [VMEM, VMEM], (VMEM, VMEM), [pltpu.VMEM((rows, features), BF16)]
    )(codes, scales)


def restore_kernel(kept, from_zl, from_a, from_both, out):
    own = (kept[...] + from_a[...].astype(F32)).astype(BF16)
    other = (from_zl[...].astype(F32) + from_both[...].astype(F32)).astype(BF16)
    spans = feature_blocks()
    for k in range(8):
        at = slice(k * 256, (k + 1) * 256)
        out[:, spans[k]] = own[:, at]
        out[:, spans[8 + k]] = other[:, at]


def restore(kept, *arrived):
    rows, half = kept.shape
    return call(restore_kernel, array((rows, 2 * half), BF16), [VMEM] * 4, VMEM)(kept, *arrived)


def token_table(rows):
    table = np.zeros((2, 4, 4, 1, 16 * rows), np.int32)
    for c, x, zh in itertools.product(range(2), range(4), range(4)):
        a, b = 1 + 2 * c, 3 - 2 * c
        at = [p * 4 + q for p in places(x, a, b) for q in places(zh, a, b)]
        table[c, x, zh, 0] = (np.array(at)[:, None] * rows + np.arange(rows)).reshape(-1)
    return table.reshape(32, 1, 16 * rows)


def arrange_kernel(table, values, out):
    source = table[lax.axis_index("dp") % 2 * 16 + lax.axis_index("tensor")]
    group = values.shape[0]
    pick = (lax.broadcasted_iota(jnp.int32, (group, group), 0) == source).astype(F32).astype(BF16)
    out[...] = lax.dot_general(
        pick, values[...], (((0,), (0,)), ((), ())), preferred_element_type=F32
    ).astype(BF16)


def arrange(values, rows):
    return call(arrange_kernel, array(values.shape, BF16), [VMEM, VMEM], VMEM)(token_table(rows), values)


def stack_kernel(*refs):
    *pieces, out, sems = refs
    copies = []
    at = 0
    for n, piece in enumerate(pieces):
        copies.append(pltpu.make_async_copy(piece, out.at[at : at + piece.shape[0]], sems.at[n]))
        at += piece.shape[0]
    for copy in copies:
        copy.start()
    for copy in copies:
        copy.wait()


def stack(*pieces):
    out = pltpu.VMEM((sum(piece.shape[0] for piece in pieces), pieces[0].shape[1]), BF16)
    return call(stack_kernel, out, [ANY] * len(pieces), VMEM, [pltpu.SemaphoreType.DMA((len(pieces),))])(*pieces)


def forward_kernel(near, away, mine, *refs):
    pieces, (rows, theirs, own, par, sems) = refs[:-5], refs[-5:]
    copies = []
    at = 0
    for n, piece in enumerate(pieces):
        copies.append(pltpu.make_async_copy(piece, theirs.at[at : at + piece.shape[0]], sems.at[n]))
        at += piece.shape[0]
    for copy in copies:
        copy.start()
    part = near.shape[0] // 4
    for n, values in enumerate((near, away)):
        for q in range(2):
            for z in range(2):
                to = (4 * z + 2 * n + q) * part
                rows[to : to + part, :] = values[(2 * q + z) * part : (2 * q + z + 1) * part, :]
    for copy in copies:
        copy.wait()
    group = own.shape[0]
    half = mine.shape[0]
    for at in range(0, mine.shape[1], TILE):
        span = slice(at, at + TILE)
        result = jnp.dot(rows[:, :half], mine[:, span], preferred_element_type=F32)
        result += jnp.dot(rows[:, half:], theirs[:, span], preferred_element_type=F32)
        own[:, span] = result[:group]
        par[:, span] = result[group:].astype(BF16)


def forward(near, away, mine, pieces):
    group, features = near.shape
    width = mine.shape[1]
    outs = (
        pltpu.VMEM((2 * group, features), BF16),
        pltpu.VMEM(mine.shape, BF16),
        pltpu.VMEM((group, width), F32),
        pltpu.VMEM((group, width), BF16),
    )
    inputs, theirs, own, par = call(
        forward_kernel,
        outs,
        [VMEM] * 3 + [ANY] * len(pieces),
        (VMEM,) * 4,
        [pltpu.SemaphoreType.DMA((len(pieces),))],
    )(near, away, mine, *pieces)
    return inputs, (mine, theirs), own, par


def gradient_kernel(own, sent, upstream, out):
    hidden = upstream.shape[1]
    stream = upstream[...].astype(F32)
    gate = own[:, :hidden] + sent[:, :hidden].astype(F32)
    up = own[:, hidden:] + sent[:, hidden:].astype(F32)
    sigmoid = jax.nn.sigmoid(gate)
    out[:, :hidden] = (stream * up * sigmoid * (1.0 + gate * (1.0 - sigmoid))).astype(BF16)
    out[:, hidden:] = (stream * gate * sigmoid).astype(BF16)


def gradient(own, sent, upstream):
    return call(gradient_kernel, array(own.shape, BF16), [VMEM] * 3, VMEM)(own, sent, upstream)


def backward_kernel(grad, mine, theirs, *refs):
    half = grad.shape[0] // 2
    if len(refs) == 3:
        before, near, away = refs
        near[:half] = before[:half]
        away[:half] = before[half:]
    for k in range(8):
        span = slice(256 * k, 256 * (k + 1))
        held = (mine, theirs)[k // 4][256 * (k % 4) : 256 * (k % 4 + 1)]
        result = lax.dot_general(
            grad[...], held, (((1,), (1,)), ((), ())), preferred_element_type=F32
        ).astype(BF16)
        if len(refs) == 3:
            near[half:, span] = result[:half]
            away[half:, span] = result[half:]
        else:
            refs[0][:, span] = result


def backward(grad, held, *before):
    out = array((grad.shape[0], 2 * held[0].shape[0]), BF16)
    outs, specs = ((out, out), (VMEM, VMEM)) if before else (out, VMEM)
    return call(backward_kernel, outs, [VMEM] * (3 + len(before)), specs)(grad, *held, *before)


def finish_kernel(scale, total, last, gate, up):
    width = gate.shape[1]
    for out, span in ((gate, slice(0, width)), (up, slice(width, 2 * width))):
        out[...] = (total[:, span] + last[:, span].astype(F32)) * scale


def finish(total, last, scale):
    rows, width = total.shape
    out = array((rows, width // 2), F32)
    return call(functools.partial(finish_kernel, scale), (out, out), [VMEM, VMEM], (VMEM, VMEM))(total, last)


def add(*values):
    total = values[0].astype(F32)
    for value in values[1:]:
        total = total + value.astype(F32)
    return total


def local(saved_codes, saved_scales, gate_weight, up_weight, hidden_grad):
    rows = saved_codes.shape[0]
    group = hidden_grad.shape[0]

    row = np.arange(8 * rows)
    taken = (row // rows % 4 * 2 + row // (4 * rows)) * rows + row % rows
    by_group = np.equal(taken[:, None], row[None, :])

    shard = join(gate_weight, up_weight)
    from_a = send(shard, Y_A)
    from_b = send(shard, Y_B)
    theirs = [send(shard, TO_CORE)]

    saved_codes, saved_scales, _ = fence(saved_codes, saved_scales, shard)
    kept, given = dequantize(saved_codes, saved_scales)
    two = jnp.concatenate([kept, send(given, TO_ZL), send(kept, ZH_A), send(given, TO_ZL_ZH_A)], axis=0)
    (two,) = fence(two)
    arrived, from_a, from_b, theirs[0] = fence(send(two, ZH_B), from_a, from_b, theirs[0])
    four = jnp.concatenate([two, arrived], axis=0)
    slab = jnp.dot(by_group.astype(BF16), four, preferred_element_type=F32).astype(BF16)
    slab, from_a = fence(slab, from_a)
    far = send(from_a, Y_B)
    near = jnp.concatenate([slab, send(slab, X_A)], axis=0)
    (near,) = fence(near)
    away = send(near, X_B)

    from_a, from_b, _ = fence(from_a, from_b, near)
    part = shard.shape[0] // 2
    theirs += [send(piece[at : at + part], TO_CORE) for piece in (from_a, from_b) for at in (0, part)]
    mine = stack(shard, from_a, from_b, far)
    far, mine = fence(far, mine)
    theirs.append(send(far, TO_CORE))
    upstream = arrange(hidden_grad, rows)

    inputs, held, own, par = forward(near, away, mine, theirs)
    sent = send(par, TO_ZL)

    grad = gradient(own, sent, upstream)
    other = send(grad, TO_ZL)
    own_back = backward(grad, held)
    other, own_back = fence(other, own_back)

    def product(first, last):
        both = jnp.concatenate([grad, other], axis=0)
        return lax.dot_general(
            inputs[:, first:last], both, (((0,), (0,)), ((), ())), preferred_element_type=F32
        )

    given = product(1536, 2048).astype(BF16)
    given, other = fence(given, other)
    shown_high = send(given, TO_CORE)
    kept, passed = backward(other, held, own_back)
    arrived = send(passed, X_B)
    shown_high, other, _ = fence(shown_high, other, kept)
    passed = add(product(512, 1024), shown_high).astype(BF16)
    from_b = send(passed, Y_B)
    other, _ = fence(other, passed)
    shown_low = send(product(1024, 1536).astype(BF16), TO_CORE)

    back = add(kept, arrived)
    half, part = group // 2, group // 4
    passed = jnp.concatenate([back[part:half], back[half + part :]], axis=0).astype(BF16)
    kept = jnp.concatenate([back[:part], back[half : half + part]], axis=0)
    four = jnp.dot(
        by_group.T.astype(np.float32),
        add(kept, send(passed, X_A)),
        preferred_element_type=F32,
        precision=lax.Precision.HIGHEST,
    )
    half = 4 * rows
    two = add(four[:half], send(four[half:].astype(BF16), ZH_B))
    kept, *passed = (two[at : at + rows] for at in range(0, half, rows))
    arrived = [send(v.astype(BF16), pairs) for v, pairs in zip(passed, (TO_ZL, ZH_A, TO_ZL_ZH_A))]
    input_grad = restore(kept, *arrived)

    passed = add(product(256, 512), shown_low[256:], from_b[256:]).astype(BF16)
    last = send(passed, Y_A)
    total = add(product(0, 256), shown_low[:256], from_b[:256])
    gate_grad, up_grad = finish(total, last, 1.0 / group)
    return input_grad, gate_grad, up_grad


def solution(mesh):
    placed = (P(BOTH, None), P(BOTH, None), P("dp", "tensor"), P("dp", "tensor"), P("dp", "tensor"))
    return jax.shard_map(
        local,
        mesh=mesh,
        in_specs=placed,
        out_specs=(P(BOTH, None), P("dp", "tensor"), P("dp", "tensor")),
        check_vma=False,
    )
```

```python
import functools
import itertools

import jax
import jax.numpy as jnp
import numpy as np
from jax import lax
from jax.experimental import pallas as pl
from jax.experimental.pallas import tpu as pltpu
from jax.sharding import PartitionSpec as P

BOTH = ("dp", "tensor")
F32 = jnp.float32
BF16 = jnp.bfloat16
FIRST, SECOND = (0, 384), (384, 896)
TILE = 256
VMEM_LIMIT = 16 * 1024 * 1024
VMEM = pl.BlockSpec(memory_space=pltpu.VMEM)
ANY = pl.BlockSpec(memory_space=pl.ANY)


def perm(target):
    def index(zl, y, c, x, zh):
        return ((zl * 4 + y) * 2 + c) * 16 + x * 4 + zh

    return [
        (index(*at), index(*target(*at, 3 if at[2] else 1, 1 if at[2] else 3)))
        for at in itertools.product(range(2), range(4), range(2), range(4), range(4))
    ]


TO_CORE = perm(lambda zl, y, c, x, zh, a, b: (zl, y, 1 - c, x, zh))
TO_ZL = perm(lambda zl, y, c, x, zh, a, b: (1 - zl, y, c, x, zh))
TO_ZL_ZH_A = perm(lambda zl, y, c, x, zh, a, b: (1 - zl, y, c, x, zh ^ a))
Y_A = perm(lambda zl, y, c, x, zh, a, b: (zl, y ^ a, c, x, zh))
Y_B = perm(lambda zl, y, c, x, zh, a, b: (zl, y ^ b, c, x, zh))
X_A = perm(lambda zl, y, c, x, zh, a, b: (zl, y, c, x ^ a, zh))
X_B = perm(lambda zl, y, c, x, zh, a, b: (zl, y, c, x ^ b, zh))
ZH_A = perm(lambda zl, y, c, x, zh, a, b: (zl, y, c, x, zh ^ a))
ZH_B = perm(lambda zl, y, c, x, zh, a, b: (zl, y, c, x, zh ^ b))


def send(value, pairs):
    return lax.ppermute(value, BOTH, pairs)


def fence(*values):
    return lax.optimization_barrier(values)


def after(value, *others):
    return lax.optimization_barrier((value, *others))[0]


def call(kernel, out_shape, in_specs, out_specs, scratch=(), cost=None):
    return pl.pallas_call(
        kernel,
        out_shape=out_shape,
        in_specs=in_specs,
        out_specs=out_specs,
        scratch_shapes=list(scratch),
        cost_estimate=cost,
        compiler_params=pltpu.CompilerParams(vmem_limit_bytes=VMEM_LIMIT),
    )


def in_vmem(value):
    return pltpu.with_memory_space_constraint(value, pltpu.VMEM)


def in_hbm(value):
    return pltpu.with_memory_space_constraint(value, pltpu.HBM)


def array(shape, dtype):
    return jax.ShapeDtypeStruct(shape, dtype)


def join_kernel(gate, up, out, sems):
    width = gate.shape[1]
    copies = [
        pltpu.make_async_copy(gate, out.at[:, :width], sems.at[0]),
        pltpu.make_async_copy(up, out.at[:, width:], sems.at[1]),
    ]
    for copy in copies:
        copy.start()
    for copy in copies:
        copy.wait()


def join(gate, up):
    rows, width = gate.shape
    return call(
        join_kernel, pltpu.VMEM((rows, 2 * width), BF16), [ANY, ANY], VMEM, [pltpu.SemaphoreType.DMA((2,))]
    )(in_hbm(gate), in_hbm(up))


def places(p, first, second):
    return (p, p ^ first, p ^ second, p ^ 2)


def feature_blocks():
    dp = lax.axis_index("dp")
    zl, y, c = dp // 8, (dp // 2) % 4, dp % 2
    a, b = 1 + 2 * c, 3 - 2 * c
    blocks = [p * 2 + c for p in places(y, a, b)] + [p * 2 + 1 - c for p in places(y, b, a)]
    starts = [(zl * 8 + k) * 256 for k in blocks] + [((1 - zl) * 8 + k) * 256 for k in blocks]
    return [pl.ds(pl.multiple_of(start, 256), 256) for start in starts]


def dequantize_kernel(codes, scales, own, other, values):
    blocks = scales.shape[1]
    width = codes.shape[1] // blocks
    for b in range(blocks):
        at = slice(b * width, (b + 1) * width)
        values[:, at] = (codes[:, at].astype(F32) * scales[:, b : b + 1].astype(F32)).astype(BF16)
    spans = feature_blocks()
    for k in range(8):
        at = slice(k * 256, (k + 1) * 256)
        own[:, at] = values[:, spans[k]]
        other[:, at] = values[:, spans[8 + k]]


def dequantize(codes, scales):
    rows, features = codes.shape
    half = array((rows, features // 2), BF16)
    return call(
        dequantize_kernel, (half, half), [VMEM, VMEM], (VMEM, VMEM), [pltpu.VMEM((rows, features), BF16)]
    )(codes, scales)


def restore_kernel(kept, from_zl, from_a, from_both, out):
    own = (kept[...] + from_a[...].astype(F32)).astype(BF16)
    other = (from_zl[...].astype(F32) + from_both[...].astype(F32)).astype(BF16)
    spans = feature_blocks()
    for k in range(8):
        at = slice(k * 256, (k + 1) * 256)
        out[:, spans[k]] = own[:, at]
        out[:, spans[8 + k]] = other[:, at]


def restore(kept, *arrived):
    rows, half = kept.shape
    return call(restore_kernel, array((rows, 2 * half), BF16), [VMEM] * 4, VMEM)(kept, *arrived)


def token_table(rows):
    table = np.zeros((2, 4, 4, 1, 16 * rows), np.int32)
    for c, x, zh in itertools.product(range(2), range(4), range(4)):
        a, b = 1 + 2 * c, 3 - 2 * c
        at = [p * 4 + q for p in places(x, a, b) for q in places(zh, a, b)]
        table[c, x, zh, 0] = (np.array(at)[:, None] * rows + np.arange(rows)).reshape(-1)
    return table.reshape(32, 1, 16 * rows)


def arrange_kernel(table, values, out):
    source = table[lax.axis_index("dp") % 2 * 16 + lax.axis_index("tensor")]
    group = values.shape[0]
    pick = (lax.broadcasted_iota(jnp.int32, (group, group), 0) == source).astype(F32).astype(BF16)
    out[...] = lax.dot_general(
        pick, values[...], (((0,), (0,)), ((), ())), preferred_element_type=F32
    ).astype(BF16)


def arrange(values, rows):
    return call(arrange_kernel, array(values.shape, BF16), [VMEM, VMEM], VMEM)(token_table(rows), values)


def stack_kernel(*refs):
    *pieces, out, sems = refs
    copies = []
    at = 0
    for n, piece in enumerate(pieces):
        copies.append(pltpu.make_async_copy(piece, out.at[at : at + piece.shape[0]], sems.at[n]))
        at += piece.shape[0]
    for copy in copies:
        copy.start()
    for copy in copies:
        copy.wait()


def stack(*pieces):
    out = pltpu.VMEM((sum(piece.shape[0] for piece in pieces), pieces[0].shape[1]), BF16)
    return call(stack_kernel, out, [ANY] * len(pieces), VMEM, [pltpu.SemaphoreType.DMA((len(pieces),))])(*pieces)


def columns_of(chunk, hidden):
    first, last = chunk
    return [slice(first, last), slice(hidden + first, hidden + last)]


def tiles_of(chunk, hidden):
    to = 0
    for span in columns_of(chunk, hidden):
        for at in range(span.start, span.stop, TILE):
            wide = min(TILE, span.stop - at)
            yield slice(at, at + wide), slice(to, to + wide)
            to += wide


def products(rows, mine, theirs, span):
    half = mine.shape[0]
    return jnp.dot(rows[:, :half], mine[:, span], preferred_element_type=F32) + jnp.dot(
        rows[:, half:], theirs[:, span], preferred_element_type=F32
    )


def first_kernel(near, away, mine, *refs):
    pieces, (rows, theirs, kept, given, sems) = refs[:-5], refs[-5:]
    copies = []
    at = 0
    for n, piece in enumerate(pieces):
        copies.append(pltpu.make_async_copy(piece, theirs.at[at : at + piece.shape[0]], sems.at[n]))
        at += piece.shape[0]
    for copy in copies:
        copy.start()
    part = near.shape[0] // 4
    for n, values in enumerate((near, away)):
        for q in range(2):
            for z in range(2):
                to = (4 * z + 2 * n + q) * part
                rows[to : to + part, :] = values[(2 * q + z) * part : (2 * q + z + 1) * part, :]
    for copy in copies:
        copy.wait()
    for span, to in tiles_of(FIRST, mine.shape[1] // 2):
        result = products(rows, mine, theirs, span)
        kept[:, to] = result
        given[:, to] = result.astype(BF16)


def first_products(near, away, mine, pieces):
    group, features = near.shape
    width = 2 * (FIRST[1] - FIRST[0])
    outs = (
        pltpu.VMEM((2 * group, features), BF16),
        pltpu.VMEM(mine.shape, BF16),
        pltpu.VMEM((2 * group, width), F32),
        pltpu.VMEM((2 * group, width), BF16),
    )
    return call(
        first_kernel,
        outs,
        [VMEM] * 3 + [ANY] * len(pieces),
        (VMEM,) * 4,
        [pltpu.SemaphoreType.DMA((len(pieces),))],
    )(near, away, mine, *pieces)


def second_kernel(rows, mine, theirs, kept, given):
    for span, to in tiles_of(SECOND, mine.shape[1] // 2):
        result = products(rows, mine, theirs, span)
        kept[:, to] = result
        given[:, to] = result.astype(BF16)


def second_products(rows, mine, theirs):
    shape = (rows.shape[0], 2 * (SECOND[1] - SECOND[0]))
    outs = (pltpu.VMEM(shape, F32), pltpu.VMEM(shape, BF16))
    return call(second_kernel, outs, [VMEM] * 3, (VMEM,) * 2)(rows, mine, theirs)


def gradient_kernel(start, kept, sent, own_stream, other_stream, out):
    rows, width = sent.shape[0] // 2, sent.shape[1] // 2
    for z, stream in enumerate((own_stream, other_stream)):
        held = slice(z * rows, (z + 1) * rows)
        came = slice((1 - z) * rows, (2 - z) * rows)
        upstream = stream[:, start : start + width].astype(F32)
        gate = kept[held, :width] + sent[came, :width].astype(F32)
        up = kept[held, width:] + sent[came, width:].astype(F32)
        sigmoid = jax.nn.sigmoid(gate)
        out[held, :width] = (upstream * up * sigmoid * (1.0 + gate * (1.0 - sigmoid))).astype(BF16)
        out[held, width:] = (upstream * gate * sigmoid).astype(BF16)


def gradient(chunk, kept, sent, own_stream, other_stream):
    return call(functools.partial(gradient_kernel, chunk[0]), array(sent.shape, BF16), [VMEM] * 4, VMEM)(
        kept, sent, own_stream, other_stream
    )


def backward_kernel(side, first, second, mine, theirs, out, grads):
    group, rows = first.shape[0] // 2, first.shape[0] // 4
    for chunk, part in ((FIRST, first), (SECOND, second)):
        width = chunk[1] - chunk[0]
        for m, span in enumerate(columns_of(chunk, mine.shape[1] // 2)):
            for z in range(2):
                at = z * group + side * rows
                grads[z * rows : (z + 1) * rows, span] = part[at : at + rows, m * width : (m + 1) * width]
    for k in range(8):
        held = (mine, theirs)[k // 4][256 * (k % 4) : 256 * (k % 4 + 1)]
        out[:, 256 * k : 256 * (k + 1)] = lax.dot_general(
            grads[...], held, (((1,), (1,)), ((), ())), preferred_element_type=F32
        ).astype(BF16)


def backward(side, first, second, mine, theirs):
    rows, width = first.shape[0] // 2, mine.shape[1]
    return call(
        functools.partial(backward_kernel, side),
        array((rows, 2 * mine.shape[0]), BF16),
        [VMEM] * 4,
        VMEM,
        [pltpu.VMEM((rows, width), BF16)],
    )(first, second, mine, theirs)


def finish_kernel(scale, first, second, first_last, second_last, gate, up):
    hidden = gate.shape[1]
    for chunk, total, last in ((FIRST, first, first_last), (SECOND, second, second_last)):
        width = chunk[1] - chunk[0]
        for m, out in enumerate((gate, up)):
            at = slice(m * width, (m + 1) * width)
            out[:, chunk[0] : chunk[1]] = (total[:, at] + last[:, at].astype(F32)) * scale


def finish(sums, lasts, scale):
    out = array((sums[0].shape[0], SECOND[1]), F32)
    return call(functools.partial(finish_kernel, scale), (out, out), [VMEM] * 4, (VMEM, VMEM))(*sums, *lasts)


def add(*values):
    total = values[0].astype(F32)
    for value in values[1:]:
        total = total + value.astype(F32)
    return total


def local(saved_codes, saved_scales, gate_weight, up_weight, hidden_grad):
    rows = saved_codes.shape[0]
    group = hidden_grad.shape[0]

    row = np.arange(8 * rows)
    taken = (row // rows % 4 * 2 + row // (4 * rows)) * rows + row % rows
    by_group = np.equal(taken[:, None], row[None, :])

    shard = join(gate_weight, up_weight)
    from_a = send(shard, Y_A)
    from_b = send(shard, Y_B)

    saved_codes, saved_scales, _ = fence(saved_codes, saved_scales, shard)
    kept, given = dequantize(saved_codes, saved_scales)
    two = jnp.concatenate([kept, send(given, TO_ZL), send(kept, ZH_A), send(given, TO_ZL_ZH_A)], axis=0)
    two, shown = fence(two, shard)
    theirs = [send(shown, TO_CORE)]
    arrived = after(send(two, ZH_B), from_a)
    four = jnp.concatenate([two, arrived], axis=0)
    slab = jnp.dot(by_group.astype(BF16), four, preferred_element_type=F32).astype(BF16)
    (slab,) = fence(slab)
    far = send(from_a, Y_B)
    arrived, from_b, theirs[0] = fence(send(slab, X_A), from_b, theirs[0])
    near = jnp.concatenate([slab, arrived], axis=0)
    (near,) = fence(near)
    away = send(near, X_B)

    both = stack(after(from_a, near), from_b)
    theirs += [send(both[at : at + 192], TO_CORE) for at in range(0, both.shape[0], 192)]
    mine = stack(shard, from_a, from_b, far)
    theirs.append(send(after(far, mine), TO_CORE))

    upstream = arrange(hidden_grad, rows)
    near, away, other_upstream = fence(near, away, send(upstream, TO_ZL))

    inputs, theirs, kept_first, given = first_products(near, away, mine, theirs)
    sent_first = send(given, TO_ZL)
    kept_second, given = second_products(inputs, mine, theirs)
    sent_second = send(given, TO_ZL)
    sent_first = after(sent_first, kept_second)
    half, part = group // 2, group // 4

    def product(first, last, grad):
        return lax.dot_general(
            inputs[:, first:last], grad, (((0,), (0,)), ((), ())), preferred_element_type=F32
        )

    def show(value):
        (value,) = fence(value.astype(BF16))
        pieces = [send(value[at : at + 128], TO_CORE) for at in range(0, value.shape[0], 128)]
        return jnp.concatenate(pieces, axis=0)

    first = gradient(FIRST, kept_first, sent_first, upstream, other_upstream)
    high = show(product(1536, 2048, first))
    passed = add(product(512, 1024, first), high).astype(BF16)
    first_b = send(passed, Y_B)

    second = gradient(SECOND, kept_second, sent_second, upstream, other_upstream)
    back_away = backward(1, first, second, mine, theirs)
    back_sent = send(back_away, X_B)
    back = backward(0, first, after(second, first_b, back_away), mine, theirs)
    first_low = send(product(1024, 1536, after(first, back_away)).astype(BF16), TO_CORE)
    second = after(second, back)
    high = show(product(1536, 2048, second))
    passed = add(product(512, 1024, second), high).astype(BF16)
    second_b = send(passed, Y_B)
    low = product(1024, 1536, after(second, passed)).astype(BF16)
    second_low = send(low, TO_CORE)
    back_sent = after(back_sent, low)

    def second_sum(grad, shown, from_b):
        return add(product(256, 512, grad), shown[256:], from_b[256:]).astype(BF16)

    def own_sum(grad, shown, from_b):
        return add(product(0, 256, grad), shown[:256], from_b[:256])

    back = add(back, back_sent)
    passed = jnp.concatenate([back[part:half], back[half + part :]], axis=0).astype(BF16)
    kept = jnp.concatenate([back[:part], back[half : half + part]], axis=0)
    arrived = send(passed, X_A)
    first_last = send(second_sum(first, first_low, first_b), Y_A)
    four = jnp.dot(
        by_group.T.astype(np.float32),
        add(kept, arrived),
        preferred_element_type=F32,
        precision=lax.Precision.HIGHEST,
    )
    part = 4 * rows
    passed = second_sum(second, second_low, second_b)
    arrived = after(send(four[part:].astype(BF16), ZH_B), first_last, passed)
    second_last = send(passed, Y_A)
    two = add(four[:part], arrived)
    kept, *passed = (two[at : at + rows] for at in range(0, part, rows))
    arrived = [send(v.astype(BF16), pairs) for v, pairs in zip(passed, (TO_ZL, ZH_A, TO_ZL_ZH_A))]
    arrived[0] = after(arrived[0], second_last)
    input_grad = restore(kept, *arrived)
    sums = [own_sum(first, first_low, first_b), own_sum(second, second_low, second_b)]
    gate_grad, up_grad = finish(sums, [first_last, second_last], 1.0 / group)
    return input_grad, gate_grad, up_grad


def solution(mesh):
    placed = (P(BOTH, None), P(BOTH, None), P("dp", "tensor"), P("dp", "tensor"), P("dp", "tensor"))
    return jax.shard_map(
        local,
        mesh=mesh,
        in_specs=placed,
        out_specs=(P(BOTH, None), P("dp", "tensor"), P("dp", "tensor")),
        check_vma=False,
    )
```

```python
import functools
import itertools

import jax
import jax.numpy as jnp
import numpy as np
from jax import lax
from jax.experimental import pallas as pl
from jax.experimental.pallas import tpu as pltpu
from jax.sharding import PartitionSpec as P

BOTH = ("dp", "tensor")
F32 = jnp.float32
BF16 = jnp.bfloat16
FIRST, SECOND = (0, 384), (384, 896)
TILE = 256
VMEM_LIMIT = 16 * 1024 * 1024
VMEM = pl.BlockSpec(memory_space=pltpu.VMEM)
ANY = pl.BlockSpec(memory_space=pl.ANY)


def perm(target):
    def index(zl, y, c, x, zh):
        return ((zl * 4 + y) * 2 + c) * 16 + x * 4 + zh

    return [
        (index(*at), index(*target(*at, 3 if at[2] else 1, 1 if at[2] else 3)))
        for at in itertools.product(range(2), range(4), range(2), range(4), range(4))
    ]


TO_CORE = perm(lambda zl, y, c, x, zh, a, b: (zl, y, 1 - c, x, zh))
TO_ZL = perm(lambda zl, y, c, x, zh, a, b: (1 - zl, y, c, x, zh))
TO_ZL_ZH_A = perm(lambda zl, y, c, x, zh, a, b: (1 - zl, y, c, x, zh ^ a))
Y_A = perm(lambda zl, y, c, x, zh, a, b: (zl, y ^ a, c, x, zh))
Y_B = perm(lambda zl, y, c, x, zh, a, b: (zl, y ^ b, c, x, zh))
X_A = perm(lambda zl, y, c, x, zh, a, b: (zl, y, c, x ^ a, zh))
X_B = perm(lambda zl, y, c, x, zh, a, b: (zl, y, c, x ^ b, zh))
ZH_A = perm(lambda zl, y, c, x, zh, a, b: (zl, y, c, x, zh ^ a))
ZH_B = perm(lambda zl, y, c, x, zh, a, b: (zl, y, c, x, zh ^ b))


def send(value, pairs):
    return lax.ppermute(value, BOTH, pairs)


def fence(*values):
    return lax.optimization_barrier(values)


def after(value, *others):
    return lax.optimization_barrier((value, *others))[0]


def call(kernel, out_shape, in_specs, out_specs, scratch=(), cost=None):
    return pl.pallas_call(
        kernel,
        out_shape=out_shape,
        in_specs=in_specs,
        out_specs=out_specs,
        scratch_shapes=list(scratch),
        cost_estimate=cost,
        compiler_params=pltpu.CompilerParams(vmem_limit_bytes=VMEM_LIMIT),
    )


def in_vmem(value):
    return pltpu.with_memory_space_constraint(value, pltpu.VMEM)


def in_hbm(value):
    return pltpu.with_memory_space_constraint(value, pltpu.HBM)


def array(shape, dtype):
    return jax.ShapeDtypeStruct(shape, dtype)


def join_kernel(gate, up, out, sems):
    width = gate.shape[1]
    copies = [
        pltpu.make_async_copy(gate, out.at[:, :width], sems.at[0]),
        pltpu.make_async_copy(up, out.at[:, width:], sems.at[1]),
    ]
    for copy in copies:
        copy.start()
    for copy in copies:
        copy.wait()


def join(gate, up):
    rows, width = gate.shape
    return call(
        join_kernel, pltpu.VMEM((rows, 2 * width), BF16), [ANY, ANY], VMEM, [pltpu.SemaphoreType.DMA((2,))]
    )(in_hbm(gate), in_hbm(up))


def places(p, first, second):
    return (p, p ^ first, p ^ second, p ^ 2)


def feature_blocks():
    dp = lax.axis_index("dp")
    zl, y, c = dp // 8, (dp // 2) % 4, dp % 2
    a, b = 1 + 2 * c, 3 - 2 * c
    blocks = [p * 2 + c for p in places(y, a, b)] + [p * 2 + 1 - c for p in places(y, b, a)]
    starts = [(zl * 8 + k) * 256 for k in blocks] + [((1 - zl) * 8 + k) * 256 for k in blocks]
    return [pl.ds(pl.multiple_of(start, 256), 256) for start in starts]


def dequantize_kernel(codes, scales, own, other, values):
    blocks = scales.shape[1]
    width = codes.shape[1] // blocks
    for b in range(blocks):
        at = slice(b * width, (b + 1) * width)
        values[:, at] = (codes[:, at].astype(F32) * scales[:, b : b + 1].astype(F32)).astype(BF16)
    spans = feature_blocks()
    for k in range(8):
        at = slice(k * 256, (k + 1) * 256)
        own[:, at] = values[:, spans[k]]
        other[:, at] = values[:, spans[8 + k]]


def dequantize(codes, scales):
    rows, features = codes.shape
    half = array((rows, features // 2), BF16)
    return call(
        dequantize_kernel, (half, half), [VMEM, VMEM], (VMEM, VMEM), [pltpu.VMEM((rows, features), BF16)]
    )(codes, scales)


def restore_kernel(kept, from_zl, from_a, from_both, out):
    own = (kept[...] + from_a[...].astype(F32)).astype(BF16)
    other = (from_zl[...].astype(F32) + from_both[...].astype(F32)).astype(BF16)
    spans = feature_blocks()
    for k in range(8):
        at = slice(k * 256, (k + 1) * 256)
        out[:, spans[k]] = own[:, at]
        out[:, spans[8 + k]] = other[:, at]


def restore(kept, *arrived):
    rows, half = kept.shape
    return call(restore_kernel, array((rows, 2 * half), BF16), [VMEM] * 4, VMEM)(kept, *arrived)


def token_table(rows):
    table = np.zeros((2, 4, 4, 1, 16 * rows), np.int32)
    for c, x, zh in itertools.product(range(2), range(4), range(4)):
        a, b = 1 + 2 * c, 3 - 2 * c
        at = [p * 4 + q for p in places(x, a, b) for q in places(zh, a, b)]
        table[c, x, zh, 0] = (np.array(at)[:, None] * rows + np.arange(rows)).reshape(-1)
    return table.reshape(32, 1, 16 * rows)


def arrange_kernel(table, values, out):
    source = table[lax.axis_index("dp") % 2 * 16 + lax.axis_index("tensor")]
    group = values.shape[0]
    pick = (lax.broadcasted_iota(jnp.int32, (group, group), 0) == source).astype(F32).astype(BF16)
    out[...] = lax.dot_general(
        pick, values[...], (((0,), (0,)), ((), ())), preferred_element_type=F32
    ).astype(BF16)


def arrange(values, rows):
    return call(arrange_kernel, array(values.shape, BF16), [VMEM, VMEM], VMEM)(token_table(rows), values)


def stack_kernel(*refs):
    *pieces, out, sems = refs
    copies = []
    at = 0
    for n, piece in enumerate(pieces):
        copies.append(pltpu.make_async_copy(piece, out.at[at : at + piece.shape[0]], sems.at[n]))
        at += piece.shape[0]
    for copy in copies:
        copy.start()
    for copy in copies:
        copy.wait()


def stack(*pieces):
    out = pltpu.VMEM((sum(piece.shape[0] for piece in pieces), pieces[0].shape[1]), BF16)
    return call(stack_kernel, out, [ANY] * len(pieces), VMEM, [pltpu.SemaphoreType.DMA((len(pieces),))])(*pieces)


def columns_of(chunk, hidden):
    first, last = chunk
    return [slice(first, last), slice(hidden + first, hidden + last)]


def tiles_of(chunk, hidden):
    to = 0
    for span in columns_of(chunk, hidden):
        for at in range(span.start, span.stop, TILE):
            wide = min(TILE, span.stop - at)
            yield slice(at, at + wide), slice(to, to + wide)
            to += wide


def products(rows, mine, theirs, span):
    half = mine.shape[0]
    return jnp.dot(rows[:, :half], mine[:, span], preferred_element_type=F32) + jnp.dot(
        rows[:, half:], theirs[:, span], preferred_element_type=F32
    )


def first_kernel(near, away, mine, *refs):
    pieces, (rows, theirs, kept, given, sems) = refs[:-5], refs[-5:]
    copies = []
    at = 0
    for n, piece in enumerate(pieces):
        copies.append(pltpu.make_async_copy(piece, theirs.at[at : at + piece.shape[0]], sems.at[n]))
        at += piece.shape[0]
    for copy in copies:
        copy.start()
    part = near.shape[0] // 4
    for n, values in enumerate((near, away)):
        for q in range(2):
            for z in range(2):
                to = (4 * z + 2 * n + q) * part
                rows[to : to + part, :] = values[(2 * q + z) * part : (2 * q + z + 1) * part, :]
    for copy in copies:
        copy.wait()
    for span, to in tiles_of(FIRST, mine.shape[1] // 2):
        result = products(rows, mine, theirs, span)
        kept[:, to] = result
        given[:, to] = result.astype(BF16)


def first_products(near, away, mine, pieces):
    group, features = near.shape
    width = 2 * (FIRST[1] - FIRST[0])
    outs = (
        pltpu.VMEM((2 * group, features), BF16),
        pltpu.VMEM(mine.shape, BF16),
        pltpu.VMEM((2 * group, width), F32),
        pltpu.VMEM((2 * group, width), BF16),
    )
    return call(
        first_kernel,
        outs,
        [VMEM] * 3 + [ANY] * len(pieces),
        (VMEM,) * 4,
        [pltpu.SemaphoreType.DMA((len(pieces),))],
    )(near, away, mine, *pieces)


def second_kernel(rows, mine, theirs, kept, given):
    for span, to in tiles_of(SECOND, mine.shape[1] // 2):
        result = products(rows, mine, theirs, span)
        kept[:, to] = result
        given[:, to] = result.astype(BF16)


def second_products(rows, mine, theirs):
    shape = (rows.shape[0], 2 * (SECOND[1] - SECOND[0]))
    outs = (pltpu.VMEM(shape, F32), pltpu.VMEM(shape, BF16))
    return call(second_kernel, outs, [VMEM] * 3, (VMEM,) * 2)(rows, mine, theirs)


def gradient_kernel(start, kept, sent, own_stream, other_stream, out):
    rows, width = sent.shape[0] // 2, sent.shape[1] // 2
    for z, stream in enumerate((own_stream, other_stream)):
        held = slice(z * rows, (z + 1) * rows)
        came = slice((1 - z) * rows, (2 - z) * rows)
        upstream = stream[:, start : start + width].astype(F32)
        gate = kept[held, :width] + sent[came, :width].astype(F32)
        up = kept[held, width:] + sent[came, width:].astype(F32)
        sigmoid = jax.nn.sigmoid(gate)
        out[held, :width] = (upstream * up * sigmoid * (1.0 + gate * (1.0 - sigmoid))).astype(BF16)
        out[held, width:] = (upstream * gate * sigmoid).astype(BF16)


def gradient(chunk, kept, sent, own_stream, other_stream):
    return call(functools.partial(gradient_kernel, chunk[0]), array(sent.shape, BF16), [VMEM] * 4, VMEM)(
        kept, sent, own_stream, other_stream
    )


def backward_kernel(side, first, second, mine, theirs, out, grads):
    group, rows = first.shape[0] // 2, first.shape[0] // 4
    for chunk, part in ((FIRST, first), (SECOND, second)):
        width = chunk[1] - chunk[0]
        for m, span in enumerate(columns_of(chunk, mine.shape[1] // 2)):
            for z in range(2):
                at = z * group + side * rows
                grads[z * rows : (z + 1) * rows, span] = part[at : at + rows, m * width : (m + 1) * width]
    for k in range(8):
        held = (mine, theirs)[k // 4][256 * (k % 4) : 256 * (k % 4 + 1)]
        out[:, 256 * k : 256 * (k + 1)] = lax.dot_general(
            grads[...], held, (((1,), (1,)), ((), ())), preferred_element_type=F32
        ).astype(BF16)


def backward(side, first, second, mine, theirs):
    rows, width = first.shape[0] // 2, mine.shape[1]
    return call(
        functools.partial(backward_kernel, side),
        array((rows, 2 * mine.shape[0]), BF16),
        [VMEM] * 4,
        VMEM,
        [pltpu.VMEM((rows, width), BF16)],
    )(first, second, mine, theirs)


def weight_kernel(first, count, inputs, grad, *refs):
    added, outs = refs[:count], refs[count:]
    for n in range(len(outs)):
        size = outs[n].shape[0]
        for at in range(0, size, 256):
            result = lax.dot_general(
                inputs[:, first + n * size + at : first + n * size + min(at + 256, size)],
                grad[...],
                (((0,), (0,)), ((), ())),
                preferred_element_type=F32,
            )
            wide = result.shape[0]
            for m in range(0, wide if added else 0, 128):
                piece = added[(at + m) // 128][...].astype(F32)
                outs[n][at + m : at + m + 128] = (result[m : m + 128] + piece).astype(BF16)
            if not added:
                outs[n][at : at + wide] = result.astype(BF16)


def weight_product(inputs, grad, first, last, added=(), size=None):
    size = size or last - first
    outs = (array((size, grad.shape[1]), BF16),) * ((last - first) // size)
    return call(
        functools.partial(weight_kernel, first, len(added)),
        outs,
        [VMEM] * (2 + len(added)),
        (VMEM,) * len(outs),
    )(inputs, grad, *added)


def part_kernel(side, first, mine, theirs, out):
    group, rows = first.shape[0] // 2, first.shape[0] // 4
    width = FIRST[1] - FIRST[0]
    spans = columns_of(FIRST, mine.shape[1] // 2)
    for k in range(8):
        held = (mine, theirs)[k // 4]
        for z in range(2):
            at = z * group + side * rows
            out[z * rows : (z + 1) * rows, 256 * k : 256 * (k + 1)] = sum(
                lax.dot_general(
                    first[at : at + rows, m * width : (m + 1) * width],
                    held[256 * (k % 4) : 256 * (k % 4 + 1), span],
                    (((1,), (1,)), ((), ())),
                    preferred_element_type=F32,
                )
                for m, span in enumerate(spans)
            )


def backward_part(side, first, mine, theirs):
    out = array((first.shape[0] // 2, 2 * mine.shape[0]), F32)
    return call(functools.partial(part_kernel, side), out, [VMEM] * 3, VMEM)(first, mine, theirs)


def rest_kernel(side, before, second, mine, theirs, out, grads):
    group, rows = second.shape[0] // 2, second.shape[0] // 4
    width = SECOND[1] - SECOND[0]
    spans = columns_of(SECOND, mine.shape[1] // 2)
    for z in range(2):
        at = z * group + side * rows
        grads[z * rows : (z + 1) * rows] = second[at : at + rows]
    for k in range(8):
        held = (mine, theirs)[k // 4]
        to = slice(256 * k, 256 * (k + 1))
        out[:, to] = sum(
            (
                lax.dot_general(
                    grads[:, m * width : (m + 1) * width],
                    held[256 * (k % 4) : 256 * (k % 4 + 1), span],
                    (((1,), (1,)), ((), ())),
                    preferred_element_type=F32,
                )
                for m, span in enumerate(spans)
            ),
            before[:, to],
        ).astype(BF16)


def backward_rest(side, before, second, mine, theirs):
    rows = second.shape[0] // 2
    return call(
        functools.partial(rest_kernel, side),
        array((rows, 2 * mine.shape[0]), BF16),
        [VMEM] * 4,
        VMEM,
        [pltpu.VMEM((rows, second.shape[1]), BF16)],
    )(before, second, mine, theirs)


def finish_kernel(scale, first, second, first_last, second_last, gate, up):
    hidden = gate.shape[1]
    for chunk, total, last in ((FIRST, first, first_last), (SECOND, second, second_last)):
        width = chunk[1] - chunk[0]
        for m, out in enumerate((gate, up)):
            at = slice(m * width, (m + 1) * width)
            out[:, chunk[0] : chunk[1]] = (total[:, at] + last[:, at].astype(F32)) * scale


def finish(sums, lasts, scale):
    out = array((sums[0].shape[0], SECOND[1]), F32)
    return call(functools.partial(finish_kernel, scale), (out, out), [VMEM] * 4, (VMEM, VMEM))(*sums, *lasts)


def add(*values):
    total = values[0].astype(F32)
    for value in values[1:]:
        total = total + value.astype(F32)
    return total


def local(saved_codes, saved_scales, gate_weight, up_weight, hidden_grad):
    rows = saved_codes.shape[0]
    group = hidden_grad.shape[0]

    row = np.arange(8 * rows)
    taken = (row // rows % 4 * 2 + row // (4 * rows)) * rows + row % rows
    by_group = np.equal(taken[:, None], row[None, :])

    shard = join(gate_weight, up_weight)
    from_a = send(shard, Y_A)
    from_b = send(shard, Y_B)

    saved_codes, saved_scales, _ = fence(saved_codes, saved_scales, shard)
    kept, given = dequantize(saved_codes, saved_scales)
    two = jnp.concatenate([kept, send(given, TO_ZL), send(kept, ZH_A), send(given, TO_ZL_ZH_A)], axis=0)
    two, shown = fence(two, shard)
    theirs = [send(shown, TO_CORE)]
    arrived = after(send(two, ZH_B), from_a)
    four = jnp.concatenate([two, arrived], axis=0)
    slab = jnp.dot(by_group.astype(BF16), four, preferred_element_type=F32).astype(BF16)
    (slab,) = fence(slab)
    far = send(from_a, Y_B)
    arrived, from_b, theirs[0] = fence(send(slab, X_A), from_b, theirs[0])
    near = jnp.concatenate([slab, arrived], axis=0)
    (near,) = fence(near)
    away = send(near, X_B)

    both = stack(after(from_a, near), from_b)
    theirs += [send(both[at : at + 192], TO_CORE) for at in range(0, both.shape[0], 192)]
    mine = stack(shard, from_a, from_b, far)
    theirs.append(send(after(far, mine), TO_CORE))

    upstream = arrange(hidden_grad, rows)
    near, away, other_upstream = fence(near, away, send(upstream, TO_ZL))

    inputs, theirs, kept_first, given = first_products(near, away, mine, theirs)
    sent_first = send(given, TO_ZL)
    kept_second, given = second_products(inputs, mine, theirs)
    sent_second = send(given, TO_ZL)
    sent_first = after(sent_first, kept_second)
    half, part = group // 2, group // 4

    def product(first, last, grad):
        return lax.dot_general(
            inputs[:, first:last], grad, (((0,), (0,)), ((), ())), preferred_element_type=F32
        )

    first = gradient(FIRST, kept_first, sent_first, upstream, other_upstream)
    high = [send(piece, TO_CORE) for piece in weight_product(inputs, first, 1536, 2048, size=128)]
    (passed,) = weight_product(inputs, first, 512, 1024, high)
    first_b = send(passed, Y_B)
    (low,) = weight_product(inputs, after(first, passed), 1024, 1536)
    first_low = send(low, TO_CORE)
    part_away = backward_part(1, after(first, low), mine, theirs)
    sent_second = after(sent_second, part_away)

    second = gradient(SECOND, kept_second, sent_second, upstream, other_upstream)
    back_away = backward_rest(1, part_away, second, mine, theirs)
    back_sent = send(back_away, X_B)
    high = weight_product(inputs, after(second, back_away), 1536, 2048, size=128)
    back = backward(0, first, after(second, first_b, *high), mine, theirs)
    high = [send(piece, TO_CORE) for piece in high]
    second = after(second, back)
    (passed,) = weight_product(inputs, second, 512, 1024, high)
    second_b = send(passed, Y_B)
    (low,) = weight_product(inputs, after(second, passed), 1024, 1536)
    second_low = send(low, TO_CORE)
    back_sent = after(back_sent, low)

    def second_sum(grad, shown, from_b):
        return add(product(256, 512, grad), shown[256:], from_b[256:]).astype(BF16)

    def own_sum(grad, shown, from_b):
        return add(product(0, 256, grad), shown[:256], from_b[:256])

    back = add(back, back_sent)
    passed = jnp.concatenate([back[part:half], back[half + part :]], axis=0).astype(BF16)
    kept = jnp.concatenate([back[:part], back[half : half + part]], axis=0)
    arrived = send(passed, X_A)
    first_last = send(second_sum(first, first_low, after(first_b, passed)), Y_A)
    four = jnp.dot(
        by_group.T.astype(np.float32),
        add(kept, arrived),
        preferred_element_type=F32,
        precision=lax.Precision.HIGHEST,
    )
    part = 4 * rows
    passed = second_sum(second, second_low, second_b)
    arrived = after(send(four[part:].astype(BF16), ZH_B), first_last, passed)
    second_last = send(passed, Y_A)
    two = add(four[:part], arrived)
    kept, *passed = (two[at : at + rows] for at in range(0, part, rows))
    arrived = [send(v.astype(BF16), pairs) for v, pairs in zip(passed, (TO_ZL, ZH_A, TO_ZL_ZH_A))]
    arrived[0] = after(arrived[0], second_last)
    input_grad = restore(kept, *arrived)
    sums = [own_sum(first, first_low, first_b), own_sum(second, second_low, second_b)]
    gate_grad, up_grad = finish(sums, [first_last, second_last], 1.0 / group)
    return input_grad, gate_grad, up_grad


def solution(mesh):
    placed = (P(BOTH, None), P(BOTH, None), P("dp", "tensor"), P("dp", "tensor"), P("dp", "tensor"))
    return jax.shard_map(
        local,
        mesh=mesh,
        in_specs=placed,
        out_specs=(P(BOTH, None), P("dp", "tensor"), P("dp", "tensor")),
        check_vma=False,
    )
```

```python
import functools
import itertools

import jax
import jax.numpy as jnp
import numpy as np
from jax import lax
from jax.experimental import pallas as pl
from jax.experimental.pallas import tpu as pltpu
from jax.sharding import PartitionSpec as P

BOTH = ("dp", "tensor")
F32 = jnp.float32
BF16 = jnp.bfloat16
FIRST, SECOND = (0, 384), (384, 896)
TILE = 256
VMEM_LIMIT = 16 * 1024 * 1024
VMEM = pl.BlockSpec(memory_space=pltpu.VMEM)
ANY = pl.BlockSpec(memory_space=pl.ANY)


def perm(target):
    def index(zl, y, c, x, zh):
        return ((zl * 4 + y) * 2 + c) * 16 + x * 4 + zh

    return [
        (index(*at), index(*target(*at, 3 if at[2] else 1, 1 if at[2] else 3)))
        for at in itertools.product(range(2), range(4), range(2), range(4), range(4))
    ]


TO_CORE = perm(lambda zl, y, c, x, zh, a, b: (zl, y, 1 - c, x, zh))
TO_ZL = perm(lambda zl, y, c, x, zh, a, b: (1 - zl, y, c, x, zh))
TO_ZL_ZH_A = perm(lambda zl, y, c, x, zh, a, b: (1 - zl, y, c, x, zh ^ a))
Y_A = perm(lambda zl, y, c, x, zh, a, b: (zl, y ^ a, c, x, zh))
Y_B = perm(lambda zl, y, c, x, zh, a, b: (zl, y ^ b, c, x, zh))
X_A = perm(lambda zl, y, c, x, zh, a, b: (zl, y, c, x ^ a, zh))
X_B = perm(lambda zl, y, c, x, zh, a, b: (zl, y, c, x ^ b, zh))
ZH_A = perm(lambda zl, y, c, x, zh, a, b: (zl, y, c, x, zh ^ a))
ZH_B = perm(lambda zl, y, c, x, zh, a, b: (zl, y, c, x, zh ^ b))


def send(value, pairs):
    return lax.ppermute(value, BOTH, pairs)


def fence(*values):
    return lax.optimization_barrier(values)


def after(value, *others):
    return lax.optimization_barrier((value, *others))[0]


def call(kernel, out_shape, in_specs, out_specs, scratch=(), cost=None):
    return pl.pallas_call(
        kernel,
        out_shape=out_shape,
        in_specs=in_specs,
        out_specs=out_specs,
        scratch_shapes=list(scratch),
        cost_estimate=cost,
        compiler_params=pltpu.CompilerParams(vmem_limit_bytes=VMEM_LIMIT),
    )


def in_vmem(value):
    return pltpu.with_memory_space_constraint(value, pltpu.VMEM)


def in_hbm(value):
    return pltpu.with_memory_space_constraint(value, pltpu.HBM)


def array(shape, dtype):
    return jax.ShapeDtypeStruct(shape, dtype)


def join_kernel(gate, up, out, sems):
    width = gate.shape[1]
    copies = [
        pltpu.make_async_copy(gate, out.at[:, :width], sems.at[0]),
        pltpu.make_async_copy(up, out.at[:, width:], sems.at[1]),
    ]
    for copy in copies:
        copy.start()
    for copy in copies:
        copy.wait()


def join(gate, up):
    rows, width = gate.shape
    return call(
        join_kernel, pltpu.VMEM((rows, 2 * width), BF16), [ANY, ANY], VMEM, [pltpu.SemaphoreType.DMA((2,))]
    )(in_hbm(gate), in_hbm(up))


def places(p, first, second):
    return (p, p ^ first, p ^ second, p ^ 2)


def feature_blocks():
    dp = lax.axis_index("dp")
    zl, y, c = dp // 8, (dp // 2) % 4, dp % 2
    a, b = 1 + 2 * c, 3 - 2 * c
    blocks = [p * 2 + c for p in places(y, a, b)] + [p * 2 + 1 - c for p in places(y, b, a)]
    starts = [(zl * 8 + k) * 256 for k in blocks] + [((1 - zl) * 8 + k) * 256 for k in blocks]
    return [pl.ds(pl.multiple_of(start, 256), 256) for start in starts]


def dequantize_kernel(codes, scales, own, other, values):
    blocks = scales.shape[1]
    width = codes.shape[1] // blocks
    for b in range(blocks):
        at = slice(b * width, (b + 1) * width)
        values[:, at] = (codes[:, at].astype(F32) * scales[:, b : b + 1].astype(F32)).astype(BF16)
    spans = feature_blocks()
    for k in range(8):
        at = slice(k * 256, (k + 1) * 256)
        own[:, at] = values[:, spans[k]]
        other[:, at] = values[:, spans[8 + k]]


def dequantize(codes, scales):
    rows, features = codes.shape
    half = array((rows, features // 2), BF16)
    return call(
        dequantize_kernel, (half, half), [VMEM, VMEM], (VMEM, VMEM), [pltpu.VMEM((rows, features), BF16)]
    )(codes, scales)


def restore_kernel(kept, from_zl, from_a, from_both, out):
    own = (kept[...] + from_a[...].astype(F32)).astype(BF16)
    other = (from_zl[...].astype(F32) + from_both[...].astype(F32)).astype(BF16)
    spans = feature_blocks()
    for k in range(8):
        at = slice(k * 256, (k + 1) * 256)
        out[:, spans[k]] = own[:, at]
        out[:, spans[8 + k]] = other[:, at]


def restore(kept, *arrived):
    rows, half = kept.shape
    return call(restore_kernel, array((rows, 2 * half), BF16), [VMEM] * 4, VMEM)(kept, *arrived)


def token_table(rows):
    table = np.zeros((2, 4, 4, 1, 16 * rows), np.int32)
    for c, x, zh in itertools.product(range(2), range(4), range(4)):
        a, b = 1 + 2 * c, 3 - 2 * c
        at = [p * 4 + q for p in places(x, a, b) for q in places(zh, a, b)]
        table[c, x, zh, 0] = (np.array(at)[:, None] * rows + np.arange(rows)).reshape(-1)
    return table.reshape(32, 1, 16 * rows)


def arrange_kernel(table, values, out):
    source = table[lax.axis_index("dp") % 2 * 16 + lax.axis_index("tensor")]
    group = values.shape[0]
    pick = (lax.broadcasted_iota(jnp.int32, (group, group), 0) == source).astype(F32).astype(BF16)
    out[...] = lax.dot_general(
        pick, values[...], (((0,), (0,)), ((), ())), preferred_element_type=F32
    ).astype(BF16)


def arrange(values, rows):
    return call(arrange_kernel, array(values.shape, BF16), [VMEM, VMEM], VMEM)(token_table(rows), values)


def stack_kernel(*refs):
    *pieces, out, sems = refs
    copies = []
    at = 0
    for n, piece in enumerate(pieces):
        copies.append(pltpu.make_async_copy(piece, out.at[at : at + piece.shape[0]], sems.at[n]))
        at += piece.shape[0]
    for copy in copies:
        copy.start()
    for copy in copies:
        copy.wait()


def stack(*pieces):
    out = pltpu.VMEM((sum(piece.shape[0] for piece in pieces), pieces[0].shape[1]), BF16)
    return call(stack_kernel, out, [ANY] * len(pieces), VMEM, [pltpu.SemaphoreType.DMA((len(pieces),))])(*pieces)


def columns_of(chunk, hidden):
    first, last = chunk
    return [slice(first, last), slice(hidden + first, hidden + last)]


def tiles_of(chunk, hidden):
    to = 0
    for span in columns_of(chunk, hidden):
        for at in range(span.start, span.stop, TILE):
            wide = min(TILE, span.stop - at)
            yield slice(at, at + wide), slice(to, to + wide)
            to += wide


def products(rows, mine, theirs, span):
    half = mine.shape[0]
    return jnp.dot(rows[:, :half], mine[:, span], preferred_element_type=F32) + jnp.dot(
        rows[:, half:], theirs[:, span], preferred_element_type=F32
    )


def first_kernel(near, away, mine, *refs):
    pieces, (rows, kept, given) = refs[:-3], refs[-3:]
    part = near.shape[0] // 4
    for n, values in enumerate((near, away)):
        for q in range(2):
            for z in range(2):
                to = (4 * z + 2 * n + q) * part
                rows[to : to + part, :] = values[(2 * q + z) * part : (2 * q + z + 1) * part, :]
    for span, to in tiles_of(FIRST, mine.shape[1] // 2):
        at = mine.shape[0]
        result = jnp.dot(rows[:, :at], mine[:, span], preferred_element_type=F32)
        for piece in pieces:
            end = at + piece.shape[0]
            result += jnp.dot(rows[:, at:end], piece[:, span], preferred_element_type=F32)
            at = end
        kept[:, to] = result
        given[:, to] = result.astype(BF16)


def first_products(near, away, mine, pieces):
    group, features = near.shape
    width = 2 * (FIRST[1] - FIRST[0])
    outs = (
        pltpu.VMEM((2 * group, features), BF16),
        pltpu.VMEM((2 * group, width), F32),
        pltpu.VMEM((2 * group, width), BF16),
    )
    return call(first_kernel, outs, [VMEM] * (3 + len(pieces)), (VMEM,) * 3)(near, away, mine, *pieces)


def second_kernel(rows, mine, theirs, kept, given):
    for span, to in tiles_of(SECOND, mine.shape[1] // 2):
        result = products(rows, mine, theirs, span)
        kept[:, to] = result
        given[:, to] = result.astype(BF16)


def second_products(rows, mine, theirs):
    shape = (rows.shape[0], 2 * (SECOND[1] - SECOND[0]))
    outs = (pltpu.VMEM(shape, F32), pltpu.VMEM(shape, BF16))
    return call(second_kernel, outs, [VMEM] * 3, (VMEM,) * 2)(rows, mine, theirs)


def gradient_kernel(start, kept, sent, own_stream, other_stream, out):
    rows, width = sent.shape[0] // 2, sent.shape[1] // 2
    for z, stream in enumerate((own_stream, other_stream)):
        held = slice(z * rows, (z + 1) * rows)
        came = slice((1 - z) * rows, (2 - z) * rows)
        upstream = stream[:, start : start + width].astype(F32)
        gate = kept[held, :width] + sent[came, :width].astype(F32)
        up = kept[held, width:] + sent[came, width:].astype(F32)
        sigmoid = jax.nn.sigmoid(gate)
        out[held, :width] = (upstream * up * sigmoid * (1.0 + gate * (1.0 - sigmoid))).astype(BF16)
        out[held, width:] = (upstream * gate * sigmoid).astype(BF16)


def gradient(chunk, kept, sent, own_stream, other_stream):
    return call(functools.partial(gradient_kernel, chunk[0]), array(sent.shape, BF16), [VMEM] * 4, VMEM)(
        kept, sent, own_stream, other_stream
    )


def backward_kernel(side, first, second, mine, theirs, out, grads):
    group, rows = first.shape[0] // 2, first.shape[0] // 4
    for chunk, part in ((FIRST, first), (SECOND, second)):
        width = chunk[1] - chunk[0]
        for m, span in enumerate(columns_of(chunk, mine.shape[1] // 2)):
            for z in range(2):
                at = z * group + side * rows
                grads[z * rows : (z + 1) * rows, span] = part[at : at + rows, m * width : (m + 1) * width]
    for k in range(8):
        held = (mine, theirs)[k // 4][256 * (k % 4) : 256 * (k % 4 + 1)]
        out[:, 256 * k : 256 * (k + 1)] = lax.dot_general(
            grads[...], held, (((1,), (1,)), ((), ())), preferred_element_type=F32
        ).astype(BF16)


def backward(side, first, second, mine, theirs):
    rows, width = first.shape[0] // 2, mine.shape[1]
    return call(
        functools.partial(backward_kernel, side),
        array((rows, 2 * mine.shape[0]), BF16),
        [VMEM] * 4,
        VMEM,
        [pltpu.VMEM((rows, width), BF16)],
    )(first, second, mine, theirs)


def weight_kernel(first, count, inputs, grad, *refs):
    added, outs = refs[:count], refs[count:]
    for n in range(len(outs)):
        size = outs[n].shape[0]
        for at in range(0, size, 256):
            result = lax.dot_general(
                inputs[:, first + n * size + at : first + n * size + min(at + 256, size)],
                grad[...],
                (((0,), (0,)), ((), ())),
                preferred_element_type=F32,
            )
            wide = result.shape[0]
            for m in range(0, wide if added else 0, 128):
                piece = added[(at + m) // 128][...].astype(F32)
                outs[n][at + m : at + m + 128] = (result[m : m + 128] + piece).astype(BF16)
            if not added:
                outs[n][at : at + wide] = result.astype(BF16)


def weight_product(inputs, grad, first, last, added=(), size=None):
    size = size or last - first
    outs = (array((size, grad.shape[1]), BF16),) * ((last - first) // size)
    return call(
        functools.partial(weight_kernel, first, len(added)),
        outs,
        [VMEM] * (2 + len(added)),
        (VMEM,) * len(outs),
    )(inputs, grad, *added)


def part_kernel(side, first, mine, theirs, out):
    group, rows = first.shape[0] // 2, first.shape[0] // 4
    width = FIRST[1] - FIRST[0]
    spans = columns_of(FIRST, mine.shape[1] // 2)
    for k in range(8):
        held = (mine, theirs)[k // 4]
        for z in range(2):
            at = z * group + side * rows
            out[z * rows : (z + 1) * rows, 256 * k : 256 * (k + 1)] = sum(
                lax.dot_general(
                    first[at : at + rows, m * width : (m + 1) * width],
                    held[256 * (k % 4) : 256 * (k % 4 + 1), span],
                    (((1,), (1,)), ((), ())),
                    preferred_element_type=F32,
                )
                for m, span in enumerate(spans)
            )


def backward_part(side, first, mine, theirs):
    out = array((first.shape[0] // 2, 2 * mine.shape[0]), F32)
    return call(functools.partial(part_kernel, side), out, [VMEM] * 3, VMEM)(first, mine, theirs)


def rest_kernel(side, before, second, mine, theirs, out, grads):
    group, rows = second.shape[0] // 2, second.shape[0] // 4
    width = SECOND[1] - SECOND[0]
    spans = columns_of(SECOND, mine.shape[1] // 2)
    for z in range(2):
        at = z * group + side * rows
        grads[z * rows : (z + 1) * rows] = second[at : at + rows]
    for k in range(8):
        held = (mine, theirs)[k // 4]
        to = slice(256 * k, 256 * (k + 1))
        out[:, to] = sum(
            (
                lax.dot_general(
                    grads[:, m * width : (m + 1) * width],
                    held[256 * (k % 4) : 256 * (k % 4 + 1), span],
                    (((1,), (1,)), ((), ())),
                    preferred_element_type=F32,
                )
                for m, span in enumerate(spans)
            ),
            before[:, to],
        ).astype(BF16)


def backward_rest(side, before, second, mine, theirs):
    rows = second.shape[0] // 2
    return call(
        functools.partial(rest_kernel, side),
        array((rows, 2 * mine.shape[0]), BF16),
        [VMEM] * 4,
        VMEM,
        [pltpu.VMEM((rows, second.shape[1]), BF16)],
    )(before, second, mine, theirs)


def finish_kernel(scale, first, second, first_last, second_last, gate, up):
    hidden = gate.shape[1]
    for chunk, total, last in ((FIRST, first, first_last), (SECOND, second, second_last)):
        width = chunk[1] - chunk[0]
        for m, out in enumerate((gate, up)):
            at = slice(m * width, (m + 1) * width)
            out[:, chunk[0] : chunk[1]] = (total[:, at] + last[:, at].astype(F32)) * scale


def finish(sums, lasts, scale):
    out = array((sums[0].shape[0], SECOND[1]), F32)
    return call(functools.partial(finish_kernel, scale), (out, out), [VMEM] * 4, (VMEM, VMEM))(*sums, *lasts)


def add(*values):
    total = values[0].astype(F32)
    for value in values[1:]:
        total = total + value.astype(F32)
    return total


def local(saved_codes, saved_scales, gate_weight, up_weight, hidden_grad):
    rows = saved_codes.shape[0]
    group = hidden_grad.shape[0]

    row = np.arange(8 * rows)
    taken = (row // rows % 4 * 2 + row // (4 * rows)) * rows + row % rows
    by_group = np.equal(taken[:, None], row[None, :])

    shard = join(gate_weight, up_weight)
    from_a = send(shard, Y_A)
    from_b = send(shard, Y_B)

    saved_codes, saved_scales, _ = fence(saved_codes, saved_scales, shard)
    kept, given = dequantize(saved_codes, saved_scales)
    two = jnp.concatenate([kept, send(given, TO_ZL), send(kept, ZH_A), send(given, TO_ZL_ZH_A)], axis=0)
    two, shown = fence(two, shard)
    theirs = [send(shown, TO_CORE)]
    arrived = after(send(two, ZH_B), from_a)
    four = jnp.concatenate([two, arrived], axis=0)
    slab = jnp.dot(by_group.astype(BF16), four, preferred_element_type=F32).astype(BF16)
    (slab,) = fence(slab)
    far = send(from_a, Y_B)
    arrived, from_b, theirs[0] = fence(send(slab, X_A), from_b, theirs[0])
    near = jnp.concatenate([slab, arrived], axis=0)
    (near,) = fence(near)
    away = send(near, X_B)

    both = stack(after(from_a, near), from_b)
    theirs += [send(both[at : at + 192], TO_CORE) for at in range(0, both.shape[0], 192)]
    mine = stack(shard, from_a, from_b, far)
    theirs.append(send(after(far, mine), TO_CORE))

    upstream = arrange(hidden_grad, rows)
    near, away, other_upstream = fence(near, away, send(upstream, TO_ZL))

    inputs, kept_first, given = first_products(near, away, mine, theirs)
    theirs = stack(after(theirs[0], given), *theirs[1:])
    sent_first = send(given, TO_ZL)
    kept_second, given = second_products(inputs, mine, theirs)
    sent_second = send(given, TO_ZL)
    sent_first = after(sent_first, kept_second)
    half, part = group // 2, group // 4

    def product(first, last, grad):
        return lax.dot_general(
            inputs[:, first:last], grad, (((0,), (0,)), ((), ())), preferred_element_type=F32
        )

    first = gradient(FIRST, kept_first, sent_first, upstream, other_upstream)
    high = [send(piece, TO_CORE) for piece in weight_product(inputs, first, 1536, 2048, size=128)]
    (passed,) = weight_product(inputs, first, 512, 1024, high)
    first_b = send(passed, Y_B)
    (low,) = weight_product(inputs, after(first, passed), 1024, 1536)
    first_low = send(low, TO_CORE)
    part_away = backward_part(1, after(first, low), mine, theirs)
    sent_second = after(sent_second, part_away)

    second = gradient(SECOND, kept_second, sent_second, upstream, other_upstream)
    back_away = backward_rest(1, part_away, second, mine, theirs)
    back_sent = send(back_away, X_B)
    high = weight_product(inputs, after(second, back_away), 1536, 2048, size=128)
    back = backward(0, first, after(second, first_b, *high), mine, theirs)
    high = [send(piece, TO_CORE) for piece in high]
    second = after(second, back)
    (passed,) = weight_product(inputs, second, 512, 1024, high)
    second_b = send(passed, Y_B)
    (low,) = weight_product(inputs, after(second, passed), 1024, 1536)
    second_low = send(low, TO_CORE)
    back_sent = after(back_sent, low)

    def second_sum(grad, shown, from_b):
        return add(product(256, 512, grad), shown[256:], from_b[256:]).astype(BF16)

    def own_sum(grad, shown, from_b):
        return add(product(0, 256, grad), shown[:256], from_b[:256])

    back = add(back, back_sent)
    passed = jnp.concatenate([back[part:half], back[half + part :]], axis=0).astype(BF16)
    kept = jnp.concatenate([back[:part], back[half : half + part]], axis=0)
    arrived = send(passed, X_A)
    first_last = send(second_sum(first, first_low, after(first_b, passed)), Y_A)
    four = jnp.dot(
        by_group.T.astype(np.float32),
        add(kept, arrived),
        preferred_element_type=F32,
        precision=lax.Precision.HIGHEST,
    )
    part = 4 * rows
    passed = second_sum(second, second_low, second_b)
    arrived = after(send(four[part:].astype(BF16), ZH_B), first_last, passed)
    second_last = send(passed, Y_A)
    two = add(four[:part], arrived)
    kept, *passed = (two[at : at + rows] for at in range(0, part, rows))
    arrived = [send(v.astype(BF16), pairs) for v, pairs in zip(passed, (TO_ZL, ZH_A, TO_ZL_ZH_A))]
    arrived[0] = after(arrived[0], second_last)
    input_grad = restore(kept, *arrived)
    sums = [own_sum(first, first_low, first_b), own_sum(second, second_low, second_b)]
    gate_grad, up_grad = finish(sums, [first_last, second_last], 1.0 / group)
    return input_grad, gate_grad, up_grad


def solution(mesh):
    placed = (P(BOTH, None), P(BOTH, None), P("dp", "tensor"), P("dp", "tensor"), P("dp", "tensor"))
    return jax.shard_map(
        local,
        mesh=mesh,
        in_specs=placed,
        out_specs=(P(BOTH, None), P("dp", "tensor"), P("dp", "tensor")),
        check_vma=False,
    )
```

```python
import functools
import itertools

import jax
import jax.numpy as jnp
import numpy as np
from jax import lax
from jax.experimental import pallas as pl
from jax.experimental.pallas import tpu as pltpu
from jax.sharding import PartitionSpec as P

BOTH = ("dp", "tensor")
F32 = jnp.float32
BF16 = jnp.bfloat16
FIRST, SECOND = (0, 384), (384, 896)
TILE = 256
VMEM_LIMIT = 16 * 1024 * 1024
VMEM = pl.BlockSpec(memory_space=pltpu.VMEM)
ANY = pl.BlockSpec(memory_space=pl.ANY)


def perm(target):
    def index(zl, y, c, x, zh):
        return ((zl * 4 + y) * 2 + c) * 16 + x * 4 + zh

    return [
        (index(*at), index(*target(*at, 3 if at[2] else 1, 1 if at[2] else 3)))
        for at in itertools.product(range(2), range(4), range(2), range(4), range(4))
    ]


TO_CORE = perm(lambda zl, y, c, x, zh, a, b: (zl, y, 1 - c, x, zh))
TO_ZL = perm(lambda zl, y, c, x, zh, a, b: (1 - zl, y, c, x, zh))
TO_ZL_ZH_A = perm(lambda zl, y, c, x, zh, a, b: (1 - zl, y, c, x, zh ^ a))
Y_A = perm(lambda zl, y, c, x, zh, a, b: (zl, y ^ a, c, x, zh))
Y_B = perm(lambda zl, y, c, x, zh, a, b: (zl, y ^ b, c, x, zh))
X_A = perm(lambda zl, y, c, x, zh, a, b: (zl, y, c, x ^ a, zh))
X_B = perm(lambda zl, y, c, x, zh, a, b: (zl, y, c, x ^ b, zh))
ZH_A = perm(lambda zl, y, c, x, zh, a, b: (zl, y, c, x, zh ^ a))
ZH_B = perm(lambda zl, y, c, x, zh, a, b: (zl, y, c, x, zh ^ b))


def send(value, pairs):
    return lax.ppermute(value, BOTH, pairs)


def fence(*values):
    return lax.optimization_barrier(values)


def after(value, *others):
    return lax.optimization_barrier((value, *others))[0]


def call(kernel, out_shape, in_specs, out_specs, scratch=(), cost=None):
    return pl.pallas_call(
        kernel,
        out_shape=out_shape,
        in_specs=in_specs,
        out_specs=out_specs,
        scratch_shapes=list(scratch),
        cost_estimate=cost,
        compiler_params=pltpu.CompilerParams(vmem_limit_bytes=VMEM_LIMIT),
    )


def in_vmem(value):
    return pltpu.with_memory_space_constraint(value, pltpu.VMEM)


def in_hbm(value):
    return pltpu.with_memory_space_constraint(value, pltpu.HBM)


def array(shape, dtype):
    return jax.ShapeDtypeStruct(shape, dtype)


def join_kernel(gate, up, out, sems):
    width = gate.shape[1]
    copies = [
        pltpu.make_async_copy(gate, out.at[:, :width], sems.at[0]),
        pltpu.make_async_copy(up, out.at[:, width:], sems.at[1]),
    ]
    for copy in copies:
        copy.start()
    for copy in copies:
        copy.wait()


def join(gate, up):
    rows, width = gate.shape
    return call(
        join_kernel, pltpu.VMEM((rows, 2 * width), BF16), [ANY, ANY], VMEM, [pltpu.SemaphoreType.DMA((2,))]
    )(in_hbm(gate), in_hbm(up))


def places(p, first, second):
    return (p, p ^ first, p ^ second, p ^ 2)


def feature_blocks():
    dp = lax.axis_index("dp")
    zl, y, c = dp // 8, (dp // 2) % 4, dp % 2
    a, b = 1 + 2 * c, 3 - 2 * c
    blocks = [p * 2 + c for p in places(y, a, b)] + [p * 2 + 1 - c for p in places(y, b, a)]
    starts = [(zl * 8 + k) * 256 for k in blocks] + [((1 - zl) * 8 + k) * 256 for k in blocks]
    return [pl.ds(pl.multiple_of(start, 256), 256) for start in starts]


def dequantize_kernel(codes, scales, own, other, values):
    blocks = scales.shape[1]
    width = codes.shape[1] // blocks
    for b in range(blocks):
        at = slice(b * width, (b + 1) * width)
        values[:, at] = (codes[:, at].astype(F32) * scales[:, b : b + 1].astype(F32)).astype(BF16)
    spans = feature_blocks()
    for k in range(8):
        at = slice(k * 256, (k + 1) * 256)
        own[:, at] = values[:, spans[k]]
        other[:, at] = values[:, spans[8 + k]]


def dequantize(codes, scales):
    rows, features = codes.shape
    half = array((rows, features // 2), BF16)
    return call(
        dequantize_kernel, (half, half), [VMEM, VMEM], (VMEM, VMEM), [pltpu.VMEM((rows, features), BF16)]
    )(codes, scales)


def restore_kernel(kept, from_zl, from_a, from_both, out):
    own = (kept[...] + from_a[...].astype(F32)).astype(BF16)
    other = (from_zl[...].astype(F32) + from_both[...].astype(F32)).astype(BF16)
    spans = feature_blocks()
    for k in range(8):
        at = slice(k * 256, (k + 1) * 256)
        out[:, spans[k]] = own[:, at]
        out[:, spans[8 + k]] = other[:, at]


def restore(kept, *arrived):
    rows, half = kept.shape
    return call(restore_kernel, array((rows, 2 * half), BF16), [VMEM] * 4, VMEM)(kept, *arrived)


def token_table(rows):
    table = np.zeros((2, 4, 4, 1, 16 * rows), np.int32)
    for c, x, zh in itertools.product(range(2), range(4), range(4)):
        a, b = 1 + 2 * c, 3 - 2 * c
        at = [p * 4 + q for p in places(x, a, b) for q in places(zh, a, b)]
        table[c, x, zh, 0] = (np.array(at)[:, None] * rows + np.arange(rows)).reshape(-1)
    return table.reshape(32, 1, 16 * rows)


def arrange_kernel(table, values, out):
    source = table[lax.axis_index("dp") % 2 * 16 + lax.axis_index("tensor")]
    group = values.shape[0]
    pick = (lax.broadcasted_iota(jnp.int32, (group, group), 0) == source).astype(F32).astype(BF16)
    out[...] = lax.dot_general(
        pick, values[...], (((0,), (0,)), ((), ())), preferred_element_type=F32
    ).astype(BF16)


def arrange(values, rows):
    return call(arrange_kernel, array(values.shape, BF16), [VMEM, VMEM], VMEM)(token_table(rows), values)


def stack_kernel(*refs):
    *pieces, out, sems = refs
    copies = []
    at = 0
    for n, piece in enumerate(pieces):
        copies.append(pltpu.make_async_copy(piece, out.at[at : at + piece.shape[0]], sems.at[n]))
        at += piece.shape[0]
    for copy in copies:
        copy.start()
    for copy in copies:
        copy.wait()


def stack(*pieces):
    out = pltpu.VMEM((sum(piece.shape[0] for piece in pieces), pieces[0].shape[1]), BF16)
    return call(stack_kernel, out, [ANY] * len(pieces), VMEM, [pltpu.SemaphoreType.DMA((len(pieces),))])(*pieces)


def columns_of(chunk, hidden):
    first, last = chunk
    return [slice(first, last), slice(hidden + first, hidden + last)]


def tiles_of(chunk, hidden):
    to = 0
    for span in columns_of(chunk, hidden):
        for at in range(span.start, span.stop, TILE):
            wide = min(TILE, span.stop - at)
            yield slice(at, at + wide), slice(to, to + wide)
            to += wide


def products(rows, mine, theirs, span):
    half = mine.shape[0]
    return jnp.dot(rows[:, :half], mine[:, span], preferred_element_type=F32) + jnp.dot(
        rows[:, half:], theirs[:, span], preferred_element_type=F32
    )


def first_kernel(near, away, mine, *refs):
    pieces, (rows, kept, given) = refs[:-3], refs[-3:]
    part = near.shape[0] // 4
    for n, values in enumerate((near, away)):
        for q in range(2):
            for z in range(2):
                to = (4 * z + 2 * n + q) * part
                rows[to : to + part, :] = values[(2 * q + z) * part : (2 * q + z + 1) * part, :]
    for span, to in tiles_of(FIRST, mine.shape[1] // 2):
        at = mine.shape[0]
        result = jnp.dot(rows[:, :at], mine[:, span], preferred_element_type=F32)
        for piece in pieces:
            end = at + piece.shape[0]
            result += jnp.dot(rows[:, at:end], piece[:, span], preferred_element_type=F32)
            at = end
        kept[:, to] = result
        given[:, to] = result.astype(BF16)


def first_products(near, away, mine, pieces):
    group, features = near.shape
    width = 2 * (FIRST[1] - FIRST[0])
    outs = (
        pltpu.VMEM((2 * group, features), BF16),
        pltpu.VMEM((2 * group, width), F32),
        pltpu.VMEM((2 * group, width), BF16),
    )
    return call(first_kernel, outs, [VMEM] * (3 + len(pieces)), (VMEM,) * 3)(near, away, mine, *pieces)


def second_kernel(rows, mine, theirs, kept, given):
    for span, to in tiles_of(SECOND, mine.shape[1] // 2):
        result = products(rows, mine, theirs, span)
        kept[:, to] = result
        given[:, to] = result.astype(BF16)


def second_products(rows, mine, theirs):
    shape = (rows.shape[0], 2 * (SECOND[1] - SECOND[0]))
    outs = (pltpu.VMEM(shape, F32), pltpu.VMEM(shape, BF16))
    return call(second_kernel, outs, [VMEM] * 3, (VMEM,) * 2)(rows, mine, theirs)


def gradient_kernel(start, kept, sent, own_stream, other_stream, out):
    rows, width = sent.shape[0] // 2, sent.shape[1] // 2
    for z, stream in enumerate((own_stream, other_stream)):
        held = slice(z * rows, (z + 1) * rows)
        came = slice((1 - z) * rows, (2 - z) * rows)
        upstream = stream[:, start : start + width].astype(F32)
        gate = kept[held, :width] + sent[came, :width].astype(F32)
        up = kept[held, width:] + sent[came, width:].astype(F32)
        sigmoid = jax.nn.sigmoid(gate)
        out[held, :width] = (upstream * up * sigmoid * (1.0 + gate * (1.0 - sigmoid))).astype(BF16)
        out[held, width:] = (upstream * gate * sigmoid).astype(BF16)


def gradient(chunk, kept, sent, own_stream, other_stream):
    return call(functools.partial(gradient_kernel, chunk[0]), array(sent.shape, BF16), [VMEM] * 4, VMEM)(
        kept, sent, own_stream, other_stream
    )


def backward_kernel(side, first, second, mine, theirs, out, grads):
    group, rows = first.shape[0] // 2, first.shape[0] // 4
    for chunk, part in ((FIRST, first), (SECOND, second)):
        width = chunk[1] - chunk[0]
        for m, span in enumerate(columns_of(chunk, mine.shape[1] // 2)):
            for z in range(2):
                at = z * group + side * rows
                grads[z * rows : (z + 1) * rows, span] = part[at : at + rows, m * width : (m + 1) * width]
    for k in range(8):
        held = (mine, theirs)[k // 4][256 * (k % 4) : 256 * (k % 4 + 1)]
        out[:, 256 * k : 256 * (k + 1)] = lax.dot_general(
            grads[...], held, (((1,), (1,)), ((), ())), preferred_element_type=F32
        ).astype(BF16)


def backward(side, first, second, mine, theirs):
    rows, width = first.shape[0] // 2, mine.shape[1]
    return call(
        functools.partial(backward_kernel, side),
        array((rows, 2 * mine.shape[0]), BF16),
        [VMEM] * 4,
        VMEM,
        [pltpu.VMEM((rows, width), BF16)],
    )(first, second, mine, theirs)


def weight_kernel(first, count, inputs, grad, *refs):
    added, outs = refs[:count], refs[count:]
    for n in range(len(outs)):
        size = outs[n].shape[0]
        for at in range(0, size, 256):
            result = lax.dot_general(
                inputs[:, first + n * size + at : first + n * size + min(at + 256, size)],
                grad[...],
                (((0,), (0,)), ((), ())),
                preferred_element_type=F32,
            )
            wide = result.shape[0]
            for m in range(0, wide if added else 0, 128):
                piece = added[(at + m) // 128][...].astype(F32)
                outs[n][at + m : at + m + 128] = (result[m : m + 128] + piece).astype(BF16)
            if not added:
                outs[n][at : at + wide] = result.astype(BF16)


def weight_product(inputs, grad, first, last, added=(), size=None):
    size = size or last - first
    outs = (array((size, grad.shape[1]), BF16),) * ((last - first) // size)
    return call(
        functools.partial(weight_kernel, first, len(added)),
        outs,
        [VMEM] * (2 + len(added)),
        (VMEM,) * len(outs),
    )(inputs, grad, *added)


def part_kernel(side, first, mine, theirs, out):
    group, rows = first.shape[0] // 2, first.shape[0] // 4
    width = FIRST[1] - FIRST[0]
    spans = columns_of(FIRST, mine.shape[1] // 2)
    for k in range(8):
        held = (mine, theirs)[k // 4]
        for z in range(2):
            at = z * group + side * rows
            out[z * rows : (z + 1) * rows, 256 * k : 256 * (k + 1)] = sum(
                lax.dot_general(
                    first[at : at + rows, m * width : (m + 1) * width],
                    held[256 * (k % 4) : 256 * (k % 4 + 1), span],
                    (((1,), (1,)), ((), ())),
                    preferred_element_type=F32,
                )
                for m, span in enumerate(spans)
            )


def backward_part(side, first, mine, theirs):
    out = array((first.shape[0] // 2, 2 * mine.shape[0]), F32)
    return call(functools.partial(part_kernel, side), out, [VMEM] * 3, VMEM)(first, mine, theirs)


def rest_kernel(side, before, second, mine, theirs, out, grads):
    group, rows = second.shape[0] // 2, second.shape[0] // 4
    width = SECOND[1] - SECOND[0]
    spans = columns_of(SECOND, mine.shape[1] // 2)
    for z in range(2):
        at = z * group + side * rows
        grads[z * rows : (z + 1) * rows] = second[at : at + rows]
    for k in range(8):
        held = (mine, theirs)[k // 4]
        to = slice(256 * k, 256 * (k + 1))
        out[:, to] = sum(
            (
                lax.dot_general(
                    grads[:, m * width : (m + 1) * width],
                    held[256 * (k % 4) : 256 * (k % 4 + 1), span],
                    (((1,), (1,)), ((), ())),
                    preferred_element_type=F32,
                )
                for m, span in enumerate(spans)
            ),
            before[:, to],
        ).astype(BF16)


def backward_rest(side, before, second, mine, theirs):
    rows = second.shape[0] // 2
    return call(
        functools.partial(rest_kernel, side),
        array((rows, 2 * mine.shape[0]), BF16),
        [VMEM] * 4,
        VMEM,
        [pltpu.VMEM((rows, second.shape[1]), BF16)],
    )(before, second, mine, theirs)


def finish_kernel(scale, first, second, first_last, second_last, gate, up):
    hidden = gate.shape[1]
    for chunk, total, last in ((FIRST, first, first_last), (SECOND, second, second_last)):
        width = chunk[1] - chunk[0]
        for m, out in enumerate((gate, up)):
            at = slice(m * width, (m + 1) * width)
            out[:, chunk[0] : chunk[1]] = (total[:, at] + last[:, at].astype(F32)) * scale


def finish(sums, lasts, scale):
    out = array((sums[0].shape[0], SECOND[1]), F32)
    return call(functools.partial(finish_kernel, scale), (out, out), [VMEM] * 4, (VMEM, VMEM))(*sums, *lasts)


def add(*values):
    total = values[0].astype(F32)
    for value in values[1:]:
        total = total + value.astype(F32)
    return total


def local(saved_codes, saved_scales, gate_weight, up_weight, hidden_grad):
    rows = saved_codes.shape[0]
    group = hidden_grad.shape[0]

    row = np.arange(8 * rows)
    taken = (row // rows % 4 * 2 + row // (4 * rows)) * rows + row % rows
    by_group = np.equal(taken[:, None], row[None, :])

    shard = join(gate_weight, up_weight)
    from_a = send(shard, Y_A)
    from_b = send(shard, Y_B)

    saved_codes, saved_scales, _ = fence(saved_codes, saved_scales, shard)
    kept, given = dequantize(saved_codes, saved_scales)
    two = jnp.concatenate([kept, send(given, TO_ZL), send(kept, ZH_A), send(given, TO_ZL_ZH_A)], axis=0)
    two, shown = fence(two, shard)
    theirs = [send(shown, TO_CORE)]
    arrived = after(send(two, ZH_B), from_a)
    four = jnp.concatenate([two, arrived], axis=0)
    slab = jnp.dot(by_group.astype(BF16), four, preferred_element_type=F32).astype(BF16)
    (slab,) = fence(slab)
    far = send(from_a, Y_B)
    arrived, from_b, theirs[0] = fence(send(slab, X_A), from_b, theirs[0])
    near = jnp.concatenate([slab, arrived], axis=0)
    (near,) = fence(near)
    away = send(near, X_B)

    both = stack(after(from_a, near), from_b)
    theirs += [send(both[at : at + 192], TO_CORE) for at in range(0, both.shape[0], 192)]
    mine = stack(shard, from_a, from_b, far)
    theirs.append(send(after(far, mine), TO_CORE))

    upstream = arrange(hidden_grad, rows)
    near, away, other_upstream = fence(near, away, send(upstream, TO_ZL))

    inputs, kept_first, given = first_products(near, away, mine, theirs)
    theirs = stack(after(theirs[0], given), *theirs[1:])
    sent_first = send(given, TO_ZL)
    kept_second, given = second_products(inputs, mine, theirs)
    sent_second = send(given, TO_ZL)
    sent_first = after(sent_first, kept_second)
    half, part = group // 2, group // 4

    def product(first, last, grad):
        return lax.dot_general(
            inputs[:, first:last], grad, (((0,), (0,)), ((), ())), preferred_element_type=F32
        )

    first = gradient(FIRST, kept_first, sent_first, upstream, other_upstream)
    high = [send(piece, TO_CORE) for piece in weight_product(inputs, first, 1536, 2048, size=128)]
    (passed,) = weight_product(inputs, first, 512, 1024, high)
    first_b = send(passed, Y_B)
    (low,) = weight_product(inputs, after(first, passed), 1024, 1536)
    first_low = send(low, TO_CORE)
    part_away = backward_part(1, after(first, low), mine, theirs)
    sent_second = after(sent_second, part_away)

    second = gradient(SECOND, kept_second, sent_second, upstream, other_upstream)
    back_away = backward_rest(1, part_away, second, mine, theirs)
    back_sent = send(back_away, X_B)
    high = weight_product(inputs, after(second, back_away), 1536, 2048, size=128)
    back = backward(0, first, after(second, first_b, *high), mine, theirs)
    high = [send(piece, TO_CORE) for piece in high]
    second = after(second, back)
    (passed,) = weight_product(inputs, second, 512, 1024, high)
    second_b = send(passed, Y_B)
    (low,) = weight_product(inputs, after(second, passed), 1024, 1536)
    second_low = send(low, TO_CORE)
    back_sent = after(back_sent, low)

    def second_sum(grad, shown, from_b):
        return add(product(256, 512, grad), shown[256:], from_b[256:]).astype(BF16)

    def own_sum(grad, shown, from_b):
        return add(product(0, 256, grad), shown[:256], from_b[:256])

    back = add(back, back_sent)
    passed = jnp.concatenate([back[part:half], back[half + part :]], axis=0).astype(BF16)
    kept = jnp.concatenate([back[:part], back[half : half + part]], axis=0)
    arrived = send(passed, X_A)
    first_last = send(second_sum(first, first_low, after(first_b, passed)), Y_A)
    four = jnp.dot(
        by_group.T.astype(np.float32),
        add(kept, arrived),
        preferred_element_type=F32,
        precision=lax.Precision.HIGH,
    )
    part = 4 * rows
    passed = second_sum(second, second_low, second_b)
    arrived = after(send(four[part:].astype(BF16), ZH_B), first_last, passed)
    second_last = send(passed, Y_A)
    two = add(four[:part], arrived)
    kept, *passed = (two[at : at + rows] for at in range(0, part, rows))
    arrived = [send(v.astype(BF16), pairs) for v, pairs in zip(passed, (TO_ZL, ZH_A, TO_ZL_ZH_A))]
    arrived[0] = after(arrived[0], second_last)
    input_grad = restore(kept, *arrived)
    sums = [own_sum(first, first_low, first_b), own_sum(second, second_low, second_b)]
    gate_grad, up_grad = finish(sums, [first_last, second_last], 1.0 / group)
    return input_grad, gate_grad, up_grad


def solution(mesh):
    placed = (P(BOTH, None), P(BOTH, None), P("dp", "tensor"), P("dp", "tensor"), P("dp", "tensor"))
    return jax.shard_map(
        local,
        mesh=mesh,
        in_specs=placed,
        out_specs=(P(BOTH, None), P("dp", "tensor"), P("dp", "tensor")),
        check_vma=False,
    )
```
